32 devices in a mesh: rep: 16 (over z, x, core), exp: 2 (over y).
Axes of the slice: x: 2, y: 2, z: 4, core: 2. Of those that a mesh axis runs over, the one named last changes fastest.
Arguments:
- tokens: float32 [128, 197, 512], P(('rep', 'exp')), may hold values from -6 to 6
- ln1_gain: float32 [2, 512], replicated, may hold values from 0.25 to 1.75
- ln1_bias: float32 [2, 512], replicated, may hold values from -1.75 to 1.75
- w_qkv: bfloat16 [2, 512, 1536], replicated, may hold values from -0.25 to 0.25
- w_attn_out: bfloat16 [2, 512, 512], replicated, may hold values from -2 to 2
- ln2_gain: float32 [2, 512], replicated, may hold values from 0.25 to 1.75
- ln2_bias: float32 [2, 512], replicated, may hold values from -1.75 to 1.75
- w_router: bfloat16 [2, 512, 8], replicated, may hold values from -0.1875 to 0.1875
- w_in: bfloat16 [2, 8, 512, 2048], P(None, 'exp'), may hold values from -0.25 to 0.25
- w_out: bfloat16 [2, 8, 2048, 512], P(None, 'exp'), may hold values from -3 to 3
- routes: int32 [2, 25216, 2], P(None, ('rep', 'exp')), may hold values from 0 to 7, all different within a row
- priority: int32 [2, 25216, 2], P(None, ('rep', 'exp')), may hold values from 0 to 1575, as said below
- cotangent: float32 [128, 197, 512], P(('rep', 'exp')), may hold values from -6 to 6
Outputs:
- block_out: float32 [128, 197, 512], P(('rep', 'exp'))
- grad_tokens: float32 [128, 197, 512], P(('rep', 'exp'))
- grad_ln1_gain: float32 [2, 512], P(None, 'exp')
- grad_ln1_bias: float32 [2, 512], P(None, 'exp')
- grad_w_qkv: float32 [2, 512, 1536], P(None, 'exp')
- grad_w_attn_out: float32 [2, 512, 512], P(None, 'exp')
- grad_ln2_gain: float32 [2, 512], P(None, 'exp')
- grad_ln2_bias: float32 [2, 512], P(None, 'exp')
- grad_w_router: float32 [2, 512, 8], P(None, 'exp')
- grad_w_in: float32 [2, 8, 512, 2048], P(None, 'exp', 'rep')
- grad_w_out: float32 [2, 8, 2048, 512], P(None, 'exp', 'rep')
The draws below stay inside these ranges and needn't reach their ends.
Inputs may be any that keep to these rules, and one draw needn't show every extreme that they name: `priority`: within each layer, the pairs of one device's 788 tokens hold each rank of 0 to 1575 once. `routes`: the two experts of a token differ.
All inputs are finite; a program needn't handle non-finite values.
Results may differ from the reference program's by a relative error of at most 0.028.
Values may be sent and summed in bfloat16 or wider, within the bound.
No kernel may reach another device: no remote copies, remote signals or barrier semaphores. Data moves between devices by JAX's collectives and lax.ppermute only.
A program may use at most 320 MiB of HBM per device.

```python
import jax
import jax.numpy as jnp
from jax import lax

D = 512
HEADS = 8
HEAD_DIM = 64
H = 2048
SEQ = 197
LAYERS = 2
IMG_DEV = 4
TOK_DEV = 788
IMAGES = 128
TOKENS = 25216
EXPERTS = 8
CAP = 197


def draw_priority(key, part):
    key = jax.random.fold_in(key, 7)
    block_count = TOKENS // TOK_DEV
    key_list = jax.random.split(key, LAYERS * block_count)

    def one_order(single_key):
        return jax.random.permutation(single_key, 2 * TOK_DEV)
    orders = jax.vmap(one_order)(key_list)
    return orders.reshape(LAYERS, TOKENS, 2).astype(jnp.int32)


def block_scale(key, dims, pieces, least, largest):
    def one(axis_at, shards_of):
        steps = jax.random.uniform(jax.random.fold_in(jax.random.fold_in(key, 6), axis_at), (shards_of,), jnp.float32, least / len(pieces), largest / len(pieces))
        return jnp.repeat(jnp.exp(steps), dims[axis_at] // shards_of).reshape((-1,) + (1,) * (len(dims) - axis_at - 1))

    level = one(*pieces[0])
    for cut in pieces[1:]:
        level = level * one(*cut)
    return level


def distinct(stream_key, rows, number_of, top, lift):
    sequence = jax.random.permutation(jax.random.fold_in(stream_key, 1), number_of)
    boost = sequence
    for power in range(3):
        boost = boost * boost // number_of
    boost = boost * lift // number_of
    chance = jax.random.randint(jax.random.fold_in(stream_key, 2), (rows, number_of), 0, 4096) + boost
    sure = jax.random.permutation(jax.random.fold_in(stream_key, 3), rows)[jnp.arange(number_of) % rows]
    chance = jnp.where(jnp.arange(rows)[:, None] == sure[None, :], 1 << 14, chance)
    score = chance * number_of + jnp.arange(number_of)
    return lax.top_k(score.astype(jnp.int32), top)[1].astype(jnp.int32)


def scatter_about(key, shape, deviation, limit, pieces=(), kind=jnp.bfloat16):
    loudness = block_scale(key, shape, pieces, -0.22, 0.18) if pieces else 1.0
    result = jax.random.normal(key, shape, jnp.float32) * deviation * loudness
    return jnp.minimum(jnp.maximum(result, -limit), limit).astype(kind)


def setup_inputs(seed: int = 0) -> dict:
    splits = jax.random.split(jax.random.key(seed), 14)
    tokens = scatter_about(splits[0], (IMAGES, SEQ, D), 1.0, 6.0, ((0, 32),), jnp.float32)
    ln1_gain = jnp.clip(1.0 + 0.15 * jax.random.normal(splits[1], (LAYERS, D), jnp.float32), 0.25, 1.75)
    ln1_bias = scatter_about(splits[2], (LAYERS, D), 0.3, 1.75, (), jnp.float32)
    w_qkv = scatter_about(splits[3], (LAYERS, D, 3 * D), D ** -0.5, 0.25)
    w_attn_out = scatter_about(splits[4], (LAYERS, D, D), (max(D // 64, 1)) ** -0.5, 2.0)
    ln2_gain = jnp.clip(1.0 + 0.15 * jax.random.normal(splits[5], (LAYERS, D), jnp.float32), 0.25, 1.75)
    ln2_bias = scatter_about(splits[6], (LAYERS, D), 0.3, 1.75, (), jnp.float32)
    w_router = scatter_about(splits[7], (LAYERS, D, EXPERTS), (2 * D) ** -0.5, 0.1875)
    w_in = scatter_about(splits[8], (LAYERS, EXPERTS, D, H), D ** -0.5, 0.25, ((1, 2),))
    w_out = scatter_about(splits[9], (LAYERS, EXPERTS, H, D), (max(H // 512, 1)) ** -0.5, 3.0, ((1, 2),))
    routes = distinct(splits[10], LAYERS * TOKENS, EXPERTS, 2, 2048).reshape((LAYERS, TOKENS, 2))
    priority = draw_priority(jax.random.fold_in(splits[13], 71), 0)
    cotangent = scatter_about(splits[12], (IMAGES, SEQ, D), 1.0, 6.0, ((0, 32),), jnp.float32)
    return dict(tokens=tokens, ln1_gain=ln1_gain, ln1_bias=ln1_bias, w_qkv=w_qkv, w_attn_out=w_attn_out, ln2_gain=ln2_gain, ln2_bias=ln2_bias, w_router=w_router, w_in=w_in, w_out=w_out, routes=routes, priority=priority, cotangent=cotangent)


@jax.custom_vjp
def low(v):
    return lax.optimization_barrier(v.astype(jnp.bfloat16)).astype(jnp.float32)

@jax.custom_vjp
def low_back(v):
    return v

def low_keep(v):
    return (low(v), None)

def low_pass(kept, grad):
    return (grad,)

def back_keep(v):
    return (v, None)

def back_low(kept, grad):
    return (low(grad),)
low.defvjp(low_keep, low_pass)
low_back.defvjp(back_keep, back_low)
EPSILON = 1e-06
PRECISE = lax.Precision.HIGHEST

def layer_norm(values, scales, shifts):
    average = lax.optimization_barrier(jnp.mean(values, axis=-1, keepdims=True))
    centred = values - average
    spread = lax.optimization_barrier(jnp.mean(centred * centred, axis=-1, keepdims=True))
    return centred * lax.rsqrt(spread + EPSILON) * scales + shifts

def slot_tables(route_block, rank_block):
    expert_ids = route_block.reshape(-1).astype(jnp.int32)
    rank_ids = rank_block.reshape(-1).astype(jnp.int32)
    matching = expert_ids[:, None] == expert_ids[None, :]
    earlier = rank_ids[None, :] < rank_ids[:, None]
    position = lax.optimization_barrier(jnp.sum(jnp.where(matching & earlier, 1, 0).astype(jnp.int32), axis=1)).astype(jnp.int32)
    kept_mask = position < CAP
    slot_index = (expert_ids * CAP + jnp.minimum(position, CAP - 1)).astype(jnp.int32)
    target = jnp.where(kept_mask, slot_index, EXPERTS * CAP).astype(jnp.int32)
    pair_ids = jnp.arange(2 * TOK_DEV, dtype=jnp.int32)
    owners = jnp.full((EXPERTS * CAP + 1,), -1, jnp.int32).at[target].set(pair_ids)
    return (slot_index, kept_mask, owners[:EXPERTS * CAP])

def attend(packed):
    queries, keys_part, values_part = packed
    scores = low_back(jnp.einsum('bqhd,bkhd->bhqk', queries, keys_part, precision=PRECISE) * HEAD_DIM ** (-0.5))
    probs_soft = jax.nn.softmax(scores, axis=-1)
    mixed = jnp.einsum('bhqk,bkhd->bqhd', low(probs_soft), values_part, precision=PRECISE)
    return low(low_back(mixed))

def expert_rows(packed):
    rows_in, w_first, w_second = packed
    pre_act = low_back(jnp.dot(rows_in, w_first, precision=PRECISE))
    activated = low(jax.nn.gelu(pre_act, approximate=False))
    return low(low_back(jnp.dot(activated, w_second, precision=PRECISE)))

def forward(tokens, ln1_gain, ln1_bias, w_qkv, w_attn_out, ln2_gain, ln2_bias, w_router, w_in, w_out, tables):
    device_count = TOKENS // TOK_DEV
    residual = tokens.reshape(TOKENS, D)
    for layer_index in range(LAYERS):
        slot_index, kept_mask, owners, route_ids = tables[layer_index]
        normed = low(layer_norm(residual, ln1_gain[layer_index], ln1_bias[layer_index]))
        joined = low(low_back(jnp.dot(normed, w_qkv[layer_index], precision=PRECISE)))
        split_heads = joined.reshape(device_count, IMG_DEV, SEQ, 3, HEADS, HEAD_DIM)
        attended = lax.map(jax.checkpoint(attend), (split_heads[:, :, :, 0], split_heads[:, :, :, 1], split_heads[:, :, :, 2]))
        residual = residual + low_back(jnp.dot(attended.reshape(TOKENS, D), w_attn_out[layer_index], precision=PRECISE))
        moe_in = low(layer_norm(residual, ln2_gain[layer_index], ln2_bias[layer_index]))
        logits = low_back(jnp.dot(moe_in, w_router[layer_index], precision=PRECISE))
        router_probs = jax.nn.softmax(logits, axis=-1)
        gate_values = jnp.take_along_axis(router_probs, route_ids, axis=1)
        blocks = moe_in.reshape(device_count, TOK_DEV, D)
        source = (jnp.maximum(owners, 0) // 2).astype(jnp.int32)
        picked_in = jnp.take_along_axis(blocks, source[:, :, None], axis=1)
        dispatched = low_back(jnp.where(owners[:, :, None] >= 0, picked_in, 0.0))
        by_expert = dispatched.reshape(device_count, EXPERTS, CAP, D).transpose(1, 0, 2, 3).reshape(EXPERTS, device_count * CAP, D)
        returned = lax.map(jax.checkpoint(expert_rows), (by_expert, w_in[layer_index], w_out[layer_index]))
        by_device = returned.reshape(EXPERTS, device_count, CAP, D).transpose(1, 0, 2, 3).reshape(device_count, EXPERTS * CAP, D)
        picked_out = jnp.take_along_axis(by_device, slot_index[:, :, None], axis=1).reshape(TOKENS, 2, D)
        weights = gate_values * kept_mask.reshape(TOKENS, 2).astype(gate_values.dtype)
        residual = residual + lax.optimization_barrier(jnp.sum(weights[:, :, None] * picked_out, axis=1))
    return residual.reshape(IMAGES, SEQ, D)

def reference(tokens, ln1_gain, ln1_bias, w_qkv, w_attn_out, ln2_gain, ln2_bias, w_router, w_in, w_out, routes, priority, cotangent):
    device_count = TOKENS // TOK_DEV
    tables = []
    for layer_index in range(LAYERS):
        route_blocks = routes[layer_index].reshape(device_count, TOK_DEV, 2)
        rank_blocks = priority[layer_index].reshape(device_count, TOK_DEV, 2)
        slot_index, kept_mask, owners = lax.map(lambda packed: slot_tables(packed[0], packed[1]), (route_blocks, rank_blocks))
        tables.append((slot_index, kept_mask, owners, routes[layer_index].astype(jnp.int32)))
    floats = (tokens, ln1_gain, ln1_bias, w_qkv.astype(jnp.float32), w_attn_out.astype(jnp.float32), ln2_gain, ln2_bias, w_router.astype(jnp.float32), w_in.astype(jnp.float32), w_out.astype(jnp.float32))

    def wrapped(*params):
        return forward(*params, tables)
    output, pull_back = jax.vjp(wrapped, *floats)
    gradients = pull_back(cotangent)
    return (output, gradients[0], gradients[1], gradients[2], gradients[3], gradients[4], gradients[5], gradients[6], gradients[7], gradients[8], gradients[9])
```

```python
from functools import partial

import jax
import jax.numpy as jnp
from jax import lax
from jax.experimental import pallas as pl
from jax.experimental.pallas import tpu as pltpu
from jax.sharding import PartitionSpec as P

HEADS = 8
HEAD_DIM = 64
EPSILON = 1e-06
LANES = 128
WIDE = 256
F32 = jnp.float32
BF16 = jnp.bfloat16
VMEM_LIMIT = 60 * 1024 * 1024


def round_up(value, multiple):
    return -(-value // multiple) * multiple


def nn(a, b):
    return lax.dot_general(a, b, (((1,), (0,)), ((), ())), preferred_element_type=F32)


def nt(a, b):
    return lax.dot_general(a, b, (((1,), (1,)), ((), ())), preferred_element_type=F32)


def tn(a, b):
    return lax.dot_general(a, b, (((0,), (0,)), ((), ())), preferred_element_type=F32)


def iota(shape, dim):
    return lax.broadcasted_iota(jnp.int32, shape, dim)


def row_to_col(row, rows):
    shape = (rows, row.shape[1])
    return jnp.sum(jnp.where(iota(shape, 0) == iota(shape, 1), row, 0.0), axis=1, keepdims=True)


def col_to_row(col, lanes):
    shape = (col.shape[0], lanes)
    return jnp.sum(jnp.where(iota(shape, 0) == iota(shape, 1), col, 0.0), axis=0, keepdims=True)


def normalized(values):
    average = jnp.mean(values, axis=-1, keepdims=True)
    centred = values - average
    spread = jnp.mean(centred * centred, axis=-1, keepdims=True)
    factor = lax.rsqrt(spread + EPSILON)
    return centred * factor, factor


def norm_back(grad, gain, xhat, factor):
    scaled = grad * gain
    mean_e = jnp.mean(scaled, axis=-1, keepdims=True)
    mean_x = jnp.mean(scaled * xhat, axis=-1, keepdims=True)
    return factor * (scaled - mean_e - xhat * mean_x)


def gelu_both(x):
    z = x * 0.7071067811865476
    size = jnp.abs(z)
    denom = 1.0 + 0.3275911 * size
    guess = pl.reciprocal(denom, approx=True)
    t = guess * (2.0 - denom * guess)
    raised = jnp.exp(-(z * z))
    poly = t * (
        0.127414796
        + t * (-0.142248368 + t * (0.7107068705 + t * (-0.7265760135 + t * 0.5307027145)))
    )
    tail = poly * raised
    phi = jnp.where(x >= 0.0, 1.0 - tail, tail)
    return x * phi, phi + x * raised * 0.3989422804014327


def route_kernel(ids, r_ref, p_ref, row_ref, col_ref, tall, wide, *, n, per, cap, cp, images, seq):
    tokens = images * seq
    bits = (2 * tokens - 1).bit_length()
    me = ids[0]
    key = (r_ref[0] << bits) + p_ref[0]
    tall[...] = jnp.full(tall.shape, -1, jnp.int32)
    tall[0:tokens, 0:2] = key
    flipped = tall[...].T
    lanes = tall.shape[0]
    slots = []
    experts = []
    for k in range(2):
        mine = flipped[k : k + 1, :]
        expert = mine >> bits
        least = expert << bits
        count = jnp.zeros((1, lanes), jnp.int32)
        for other in range(2):
            theirs = key[:, other : other + 1]
            hit = jnp.logical_and(theirs >= least, theirs < mine)
            count = count + jnp.sum(jnp.where(hit, 1, 0), axis=0, keepdims=True)
        group = jnp.zeros((1, lanes), jnp.int32)
        for q in range(1, n):
            group = group + jnp.where(expert >= q * per, 1, 0)
        ahead = group - me
        ahead = jnp.where(ahead < 0, ahead + n, ahead)
        slot = (ahead * per + (expert - group * per)) * cp + count
        kept = count < cap
        slots.append(jnp.where(kept, slot, -1))
        experts.append(jnp.where(kept, expert, -1))
    table = jnp.concatenate(slots + experts + [jnp.full((4, lanes), -1, jnp.int32)], axis=0)
    sp = col_ref.shape[2]
    for i in range(images):
        moved = table if i == 0 else pltpu.roll(table, lanes - seq * i, axis=1)
        piece = moved[:, :WIDE]
        piece = jnp.where(iota(piece.shape, 1) < seq, piece, -1)
        row_ref[0, :, i * WIDE : (i + 1) * WIDE] = piece
        wide[0:8, :] = piece
        col_ref[0, i] = wide[...].T[0:sp, :]


def spread_rows(me, row_ref, rhs, outs, n, per, cp, width, experts):
    slots0 = row_ref[0, 0:1, :]
    slots1 = row_ref[0, 1:2, :]
    shape = (per * cp, row_ref.shape[2])
    for d in list(range(1, n)) + [0]:
        place = iota(shape, 0) + d * per * cp
        pick = jnp.where(jnp.logical_or(place == slots0, place == slots1), 1.0, 0.0).astype(BF16)
        rows = nn(pick, rhs[...])
        base = lax.rem(me + d, n) * per
        for j in range(per):
            part = rows[j * cp : (j + 1) * cp, :]
            data = part[:, :width]
            if experts:
                both = part[:, width : width + LANES] + part[:, width + LANES :]
                gate = jnp.sum(
                    jnp.where(iota(both.shape, 1) == base + j, both, 0.0), axis=1, keepdims=True
                )
                line = col_to_row(gate, width)
                high = line.astype(BF16).astype(F32)
                where = iota(data.shape, 0)
                data = jnp.where(where == cp - 1, high, data)
                data = jnp.where(where == cp - 2, line - high, data)
            outs[d][j][...] = data.astype(BF16)


def gathered(c0, c1, v0, v1, back, n, per, cp):
    shape = (c0.shape[0], cp)
    place = iota(shape, 1)
    total = None
    for d in range(n):
        for j in range(per):
            base = (d * per + j) * cp
            pick = jnp.where(c0 - base == place, v0, 0.0) + jnp.where(c1 - base == place, v1, 0.0)
            term = nn(pick.astype(BF16), back[d][j][...])
            total = term if total is None else total + term
    return total


def take(it, n, per):
    return [[next(it) for _ in range(per)] for _ in range(n)]


def head_masks():
    lane = iota((1, LANES), 1)
    low = jnp.where(lane < HEAD_DIM, 1.0, 0.0).astype(BF16)
    high = jnp.where(lane < HEAD_DIM, 0.0, 1.0).astype(BF16)
    return low, high


def forward_kernel(*refs, first, layer, n, per, cp, images, seq, experts):
    it = iter(refs)
    ids = next(it)
    if first:
        x_ref = next(it)
    else:
        mid_in, gate_in, col_in = next(it), next(it), next(it)
        back = take(it, n, per)
    g1, b1, wqkv, wo, g2, b2, wr, col, row = (next(it) for _ in range(9))
    if not first:
        state_out = next(it)
    joined_out, probs_out, attended_out, middle_out, moe_out, rp_out, gate_out = (
        next(it) for _ in range(7)
    )
    disp = take(it, n, per)
    rhs = next(it)
    i = pl.program_id(0)
    sp = middle_out.shape[1]
    width = middle_out.shape[2]

    @pl.when(i == 0)
    def _():
        rhs[...] = jnp.zeros(rhs.shape, BF16)

    if first:
        xs = next(it)

        @pl.when(i == 0)
        def _():
            xs[...] = jnp.zeros(xs.shape, F32)

        xs[0:seq, :] = x_ref[0]
        state = xs[...]
    else:
        state = mid_in[0] + gathered(
            col_in[0, 0, :, 0:1],
            col_in[0, 0, :, 1:2],
            gate_in[0, :, 0:1],
            gate_in[0, :, 1:2],
            back,
            n,
            per,
            cp,
        )
        state_out[0] = state
    xhat, _ = normalized(state)
    normed = (xhat * g1[layer : layer + 1, :] + b1[layer : layer + 1, :]).astype(BF16)
    joined = nn(normed, wqkv[0]).astype(BF16)
    joined_out[0] = joined
    masks = head_masks()
    valid = iota((1, sp), 1) < seq
    pieces = []
    for pair in range(HEADS // 2):
        at = pair * LANES
        q = joined[:, at : at + LANES]
        k = joined[:, width + at : width + at + LANES]
        v = joined[:, 2 * width + at : 2 * width + at + LANES]
        mixed = None
        for half in range(2):
            scores = jnp.where(valid, nt(q, k * masks[half]), -1e30)
            top = jnp.max(scores, axis=-1, keepdims=True)
            raised = jnp.exp((scores - top) * HEAD_DIM ** (-0.5))
            total = jnp.sum(raised, axis=-1, keepdims=True)
            probs = (raised * (1.0 / total)).astype(BF16)
            probs_out[0, 2 * pair + half] = probs
            term = nn(probs, v * masks[half])
            mixed = term if mixed is None else mixed + term
        pieces.append(mixed.astype(BF16))
    attended = jnp.concatenate(pieces, axis=1)
    attended_out[0] = attended
    middle = state + nn(attended, wo[0])
    middle_out[0] = middle
    xhat, _ = normalized(middle)
    moe_in = (xhat * g2[layer : layer + 1, :] + b2[layer : layer + 1, :]).astype(BF16)
    moe_out[0] = moe_in
    logits = nn(moe_in, wr[0])
    lane = iota(logits.shape, 1)
    logits = jnp.where(lane < experts, logits, -1e30)
    raised = jnp.exp(logits - jnp.max(logits, axis=-1, keepdims=True))
    router = raised * (1.0 / jnp.sum(raised, axis=-1, keepdims=True))
    rp_out[0] = router
    gates = []
    for k in range(2):
        chosen = col[0, 0, :, 2 + k : 3 + k]
        gates.append(jnp.sum(jnp.where(lane == chosen, router, 0.0), axis=1, keepdims=True))
    gate_out[0] = jnp.where(lane == 0, gates[0], jnp.where(lane == 1, gates[1], 0.0))
    high = router.astype(BF16)
    low = (router - high.astype(F32)).astype(BF16)
    at = pl.multiple_of(i * WIDE, WIDE)
    rhs[pl.ds(at, sp), 0:width] = moe_in
    rhs[pl.ds(at, sp), width : width + LANES] = high
    rhs[pl.ds(at, sp), width + LANES : width + 2 * LANES] = low

    @pl.when(i == images - 1)
    def _():
        spread_rows(ids[0], row, rhs, disp, n, per, cp, width, experts)


def cotangent_kernel(*refs, n, per, cp, images, seq):
    it = iter(refs)
    ids, g_ref, row = next(it), next(it), next(it)
    outs = take(it, n, per)
    rhs = next(it)
    rhs[...] = jnp.zeros(rhs.shape, BF16)
    for i in range(images):
        rhs[i * WIDE : i * WIDE + seq, :] = g_ref[i].astype(BF16)
    spread_rows(ids[0], row, rhs, outs, n, per, cp, rhs.shape[1], 0)


def out_kernel(*refs, n, per, cp, seq):
    it = iter(refs)
    mid, gate, col = next(it), next(it), next(it)
    back = take(it, n, per)
    out = next(it)
    state = mid[0] + gathered(
        col[0, 0, :, 0:1], col[0, 0, :, 1:2], gate[0, :, 0:1], gate[0, :, 1:2], back, n, per, cp
    )
    out[0] = state[0:seq, :]


def expert_kernel(*refs, n, cp, tiles, forward, backward, sizes):
    it = iter(refs)
    ids = next(it)
    xs = [next(it) for _ in range(n)]
    if backward:
        gs = [next(it) for _ in range(n)]
        if not forward:
            made = [next(it) for _ in range(n)]
            act_in, slope_in = next(it), next(it)
    w_in, w_out = next(it), next(it)
    if forward:
        prod = [next(it) for _ in range(n)]
        if not backward:
            act_out, slope_out = next(it), next(it)
    if backward:
        dx = [next(it) for _ in range(n)]
        wire = next(it)
    xcat = next(it)
    if forward:
        acc_p = next(it)
    if backward:
        dprod, acc_d = next(it), next(it)
    h = pl.program_id(0)
    width = xcat.shape[1]

    @pl.when(h == 0)
    def _():
        for d in range(n):
            xcat[d * cp : (d + 1) * cp, :] = xs[d][...]
            if backward:
                tail = xs[d][cp - 16 : cp, 0:WIDE].astype(F32)
                line = jnp.sum(jnp.where(iota(tail.shape, 0) >= 14, tail, 0.0), axis=0, keepdims=True)
                gate = row_to_col(line, cp)
                dprod[d * cp : (d + 1) * cp, :] = (gate * gs[d][...].astype(F32)).astype(BF16)

    if forward:
        pre = nn(xcat[...], w_in[0, 0])
        value, slope = gelu_both(pre)
        act = value.astype(BF16)
        if not backward:
            act_out[...] = act
            slope_out[...] = slope.astype(BF16)
        term = nn(act, w_out[0, 0])

        @pl.when(h == 0)
        def _():
            acc_p[...] = term

        @pl.when(h > 0)
        def _():
            acc_p[...] += term
    else:
        act = act_in[...]
        slope = slope_in[...].astype(F32)
    if backward:
        zs, xs_, cores, rows_in, rows_out = sizes
        core = ids[1]
        d_act = nt(dprod[...], w_out[0, 0])
        d_pre = (d_act * slope).astype(BF16)
        grad_out = tn(act, dprod[...]).astype(BF16)
        for x in range(xs_):
            for c in range(cores):
                at = (x * cores + c) * rows_out
                wire[lax.rem(c + core, cores), x, h, tiles * rows_in :, :] = grad_out[
                    at : at + rows_out, :
                ]
        grad_in = tn(xcat[...], d_pre).astype(BF16)
        spot = pl.multiple_of(h * rows_in, rows_in)
        for z in range(zs):
            for x in range(xs_):
                for c in range(cores):
                    at = ((z * xs_ + x) * cores + c) * rows_in
                    wire[lax.rem(c + core, cores), x, z, pl.ds(spot, rows_in), :] = grad_in[
                        at : at + rows_in, :
                    ]
        term_d = nt(d_pre, w_in[0, 0])

        @pl.when(h == 0)
        def _():
            acc_d[...] = term_d

        @pl.when(h > 0)
        def _():
            acc_d[...] += term_d

    @pl.when(h == tiles - 1)
    def _():
        for d in range(n):
            rows = pl.ds(d * cp, cp)
            if forward:
                result = acc_p[rows, :].astype(BF16)
                prod[d][...] = result
            if backward:
                if not forward:
                    result = made[d][...]
                d_gate = jnp.sum(
                    result.astype(F32) * gs[d][...].astype(F32), axis=1, keepdims=True
                )
                line = col_to_row(d_gate, width)
                data = acc_d[rows, :]
                dx[d][...] = jnp.where(iota(data.shape, 0) == cp - 1, line, data).astype(BF16)


def backward_kernel(*refs, first, last, layer, n, per, cp, images, seq, experts):
    it = iter(refs)
    ids, g_ref, s_ref = next(it), next(it), next(it)
    joined_in, probs_in, attended_in, middle_in, moe_in, rp_in, col = (next(it) for _ in range(7))
    back = take(it, n, per)
    g1, b1, wqkv, wo, g2, wr = (next(it) for _ in range(6))
    if not first:
        row = next(it)
    g_out, dense = next(it), next(it)
    if not first:
        outs = take(it, n, per)
    d_cols, a_qkv, a_out, a_router, stats, flip, d_join = (next(it) for _ in range(7))
    if last:
        g_pad = next(it)
    if first:
        s_pad = next(it)
    else:
        rhs = next(it)
    i = pl.program_id(0)
    sp = middle_in.shape[1]
    width = middle_in.shape[2]
    me = ids[0]

    @pl.when(i == 0)
    def _():
        a_qkv[...] = jnp.zeros(a_qkv.shape, F32)
        a_out[...] = jnp.zeros(a_out.shape, F32)
        a_router[...] = jnp.zeros(a_router.shape, F32)
        stats[...] = jnp.zeros(stats.shape, F32)
        flip[...] = jnp.zeros(flip.shape, F32)
        if last:
            g_pad[...] = jnp.zeros(g_pad.shape, F32)
        if first:
            s_pad[...] = jnp.zeros(s_pad.shape, F32)
        else:
            rhs[...] = jnp.zeros(rhs.shape, BF16)
        for d in range(n):
            base = lax.rem(me + d, n) * per
            for j in range(per):
                tail = back[d][j][cp - 16 : cp, 0:WIDE].astype(F32)
                line = jnp.sum(jnp.where(iota(tail.shape, 0) == 15, tail, 0.0), axis=0, keepdims=True)
                column = row_to_col(line, cp)
                d_cols[d, j] = jnp.where(iota((cp, LANES), 1) == base + j, column, 0.0).astype(BF16)

    if last:
        g_pad[0:seq, :] = g_ref[0]
        g = g_pad[...]
    else:
        g = g_ref[0]
    if first:
        s_pad[0:seq, :] = s_ref[0]
        state = s_pad[...]
    else:
        state = s_ref[0]

    c0 = col[0, 0, :, 0:1]
    c1 = col[0, 0, :, 1:2]
    place = iota((sp, cp), 1)
    d_moe = None
    d_rp = None
    for d in range(n):
        for j in range(per):
            base = (d * per + j) * cp
            pick = jnp.where(jnp.logical_or(c0 - base == place, c1 - base == place), 1.0, 0.0)
            pick = pick.astype(BF16)
            term = nn(pick, back[d][j][...])
            small = nn(pick, d_cols[d, j])
            d_moe = term if d_moe is None else d_moe + term
            d_rp = small if d_rp is None else d_rp + small
    router = rp_in[0]
    d_logits = router * (d_rp - jnp.sum(d_rp * router, axis=-1, keepdims=True))
    d_logits = d_logits.astype(BF16)
    a_router[...] += tn(moe_in[0], d_logits)
    d_moe = d_moe + nt(d_logits, wr[0])
    xhat, factor = normalized(middle_in[0])
    stats[2:3, :] += jnp.sum(d_moe * xhat, axis=0, keepdims=True)
    stats[3:4, :] += jnp.sum(d_moe, axis=0, keepdims=True)
    d_middle = g + norm_back(d_moe, g2[layer : layer + 1, :], xhat, factor)
    d_branch = d_middle.astype(BF16)
    a_out[...] += tn(attended_in[0], d_branch)
    d_att = nt(d_branch, wo[0]).astype(BF16)
    masks = head_masks()
    scale = HEAD_DIM ** (-0.5)
    for pair in range(HEADS // 2):
        at = pair * LANES
        q = joined_in[0, :, at : at + LANES]
        k = joined_in[0, :, width + at : width + at + LANES]
        v = joined_in[0, :, 2 * width + at : 2 * width + at + LANES]
        do = d_att[:, at : at + LANES]
        dq = dk = dv = None
        for half in range(2):
            low = probs_in[0, 2 * pair + half]
            probs = low.astype(F32)
            dp = nt(do, v * masks[half])
            ds = (probs * (dp - jnp.sum(dp * probs, axis=-1, keepdims=True))).astype(BF16)
            terms = (
                nn(ds, k * masks[half]),
                tn(ds, q * masks[half]),
                tn(low, do * masks[half]),
            )
            if half == 0:
                dq, dk, dv = terms
            else:
                dq, dk, dv = dq + terms[0], dk + terms[1], dv + terms[2]
        d_join[:, at : at + LANES] = (dq * scale).astype(BF16)
        d_join[:, width + at : width + at + LANES] = (dk * scale).astype(BF16)
        d_join[:, 2 * width + at : 2 * width + at + LANES] = dv.astype(BF16)
    xhat, factor = normalized(state)
    normed = (xhat * g1[layer : layer + 1, :] + b1[layer : layer + 1, :]).astype(BF16)
    a_qkv[...] += tn(normed, d_join[...])
    d_normed = nt(d_join[...], wqkv[0])
    stats[0:1, :] += jnp.sum(d_normed * xhat, axis=0, keepdims=True)
    stats[1:2, :] += jnp.sum(d_normed, axis=0, keepdims=True)
    result = d_middle + norm_back(d_normed, g1[layer : layer + 1, :], xhat, factor)
    if first:
        g_out[0] = result[0:seq, :]
    else:
        g_out[0] = result
        rhs[pl.ds(pl.multiple_of(i * WIDE, WIDE), sp), :] = result.astype(BF16)

    @pl.when(i == images - 1)
    def _():
        if not first:
            spread_rows(me, row, rhs, outs, n, per, cp, width, 0)
        flip[experts : experts + 8, :] = stats[...]
        dense[:, 0 : 3 * width] = a_qkv[...].astype(BF16)
        dense[:, 3 * width : 4 * width] = a_out[...].astype(BF16)
        dense[:, 4 * width :] = (a_router[...] + flip[...].T).astype(BF16)


def spec(shape, index):
    return pl.BlockSpec(shape, index)


def whole(array):
    zeros = (0,) * len(array.shape)
    return pl.BlockSpec(tuple(array.shape), lambda *_: zeros)


def smem():
    return pl.BlockSpec(memory_space=pltpu.SMEM)


def shape_of(shape, dtype):
    return jax.ShapeDtypeStruct(tuple(shape), dtype)


def cost(flops, moved, special=0):
    return pl.CostEstimate(flops=int(flops), bytes_accessed=int(moved), transcendentals=int(special))


def per_image(shape):
    rest = (0,) * (len(shape) - 1)
    return pl.BlockSpec((1,) + tuple(shape[1:]), lambda i: (i,) + rest)


def of_layer(array, layer):
    rest = (0,) * (len(array.shape) - 1)
    return pl.BlockSpec((1,) + tuple(array.shape[1:]), lambda *_: (layer,) + rest)


def pairs_along(stride, length, total, valid, step):
    pairs = []
    for source in range(total):
        spot = (source // stride) % length
        target = spot + step
        if 0 <= target < length and valid(spot):
            pairs.append((source, source + step * stride))
    return pairs


def line_sum(parts, axis, stride, length, total, spot):
    def part(at):
        return lax.dynamic_index_in_dim(parts, jnp.clip(at, 0, length - 1), 0, keepdims=False).astype(
            F32
        )

    if length == 2:
        swap = pairs_along(stride, length, total, lambda s: True, 1) + pairs_along(
            stride, length, total, lambda s: True, -1
        )
        got = lax.ppermute(part(1 - spot).astype(BF16), axis, swap)
        return part(spot) + got.astype(F32)
    rising = part(length - 1 + spot)
    falling = part(1 - length + spot)
    for step in range(1, length):
        up = pairs_along(stride, length, total, lambda s: s <= step - 1, 1)
        down = pairs_along(stride, length, total, lambda s: length - 1 - s <= step - 1, -1)
        got_up = lax.ppermute(rising.astype(BF16), axis, up).astype(F32)
        got_down = lax.ppermute(falling.astype(BF16), axis, down).astype(F32)
        if step < length - 1:
            rising = got_up + part(length - step - 1 + spot)
            falling = got_down + part(step + 1 - length + spot)
    return part(spot) + got_up + got_down


def expert_sum(wire, rep_sizes):
    zs, xs, cores = rep_sizes
    total = zs * xs * cores
    index = lax.axis_index("rep")
    core_swap = [(r, r ^ 1) for r in range(total)]
    got = lax.ppermute(wire[1], "rep", core_swap)
    both = (wire[0].astype(F32) + got.astype(F32)).astype(BF16)
    along_x = line_sum(both, "rep", cores, xs, total, (index // cores) % xs).astype(BF16)
    return line_sum(along_x, "rep", cores * xs, zs, total, index // (cores * xs))


def local(
    tokens,
    ln1_gain,
    ln1_bias,
    w_qkv,
    w_attn_out,
    ln2_gain,
    ln2_bias,
    w_router,
    w_in,
    w_out,
    routes,
    priority,
    cotangent,
    n,
    reps,
):
    images, seq, width = tokens.shape
    tok_count = images * seq
    layers, per, _, hidden = w_in.shape
    experts = n * per
    cap = 2 * tok_count // experts
    cp = round_up(cap + 2, 16)
    sp = round_up(seq, 16)
    zs, cores = 4, 2
    xs = reps // (zs * cores)
    rep_sizes = (zs, xs, cores)
    tiles = zs
    tile = hidden // tiles
    rows_in = width // reps
    rows_out = hidden // reps
    rows = tiles * rows_in + rows_out
    me = lax.axis_index("exp")
    core = lax.axis_index("rep") % cores
    ids = jnp.stack([me, core]).astype(jnp.int32)
    router_wide = jnp.pad(w_router, ((0, 0), (0, 0), (0, LANES - experts)))
    params = pltpu.CompilerParams(
        vmem_limit_bytes=VMEM_LIMIT, dimension_semantics=("arbitrary",)
    )
    dims = dict(n=n, per=per, cp=cp)

    lanes = round_up(tok_count, LANES)
    row, col = pl.pallas_call(
        partial(route_kernel, cap=cap, images=images, seq=seq, **dims),
        grid=(layers,),
        in_specs=[smem()] + [spec((1, tok_count, 2), lambda l: (l, 0, 0))] * 2,
        out_specs=[
            spec((1, 8, images * WIDE), lambda l: (l, 0, 0)),
            spec((1, images, sp, LANES), lambda l: (l, 0, 0, 0)),
        ],
        out_shape=[
            shape_of((layers, 8, images * WIDE), jnp.int32),
            shape_of((layers, images, sp, LANES), jnp.int32),
        ],
        scratch_shapes=[pltpu.VMEM((lanes, LANES), jnp.int32), pltpu.VMEM((LANES, WIDE), jnp.int32)],
        compiler_params=params,
        cost_estimate=cost(4e7, 1e6),
        name="route",
    )(ids, routes, priority)

    slot_shape = shape_of((cp, width), BF16)
    slot_shapes = [slot_shape] * (n * per)
    slot_specs = [whole(slot_shape)] * (n * per)

    def nested(flat):
        return [list(flat[d * per : (d + 1) * per]) for d in range(n)]

    def flat_of(lists):
        return [part for group in lists for part in group]

    def send(lists):
        result = [lists[0]]
        for d in range(1, n):
            pairs = [(s, (s + d) % n) for s in range(n)]
            result.append([lax.ppermute(part, "exp", pairs) for part in lists[d]])
        return result

    def send_back(lists):
        result = [lists[0]]
        for d in range(1, n):
            pairs = [(s, (s - d) % n) for s in range(n)]
            result.append([lax.ppermute(part, "exp", pairs) for part in lists[d]])
        return result

    def col_spec(layer):
        return spec((1, 1, sp, LANES), lambda i: (layer, i, 0, 0))

    row_spec_of = lambda layer: spec((1, 8, images * WIDE), lambda *_: (layer, 0, 0))

    top = layers - 1
    g_rows = nested(
        pl.pallas_call(
            partial(cotangent_kernel, images=images, seq=seq, **dims),
            grid=(1,),
            in_specs=[smem(), whole(cotangent), row_spec_of(top)],
            out_specs=slot_specs,
            out_shape=slot_shapes,
            scratch_shapes=[pltpu.VMEM((images * WIDE, width), BF16)],
            compiler_params=params,
            cost_estimate=cost(4 * n * per * cp * images * WIDE * width // 2, 4e6),
            name="spread_cotangent",
        )(ids, cotangent, row)
    )
    g_rows = send(g_rows)

    def run_forward(layer, previous):
        first = layer == 0
        args = [ids]
        specs = [smem()]
        if first:
            args += [tokens]
            specs += [per_image(tokens.shape)]
        else:
            middle, gate, back = previous
            args += [middle, gate, col] + flat_of(back)
            specs += [per_image(middle.shape), per_image(gate.shape), col_spec(layer - 1)] + slot_specs
        args += [ln1_gain, ln1_bias, w_qkv, w_attn_out, ln2_gain, ln2_bias, router_wide, col, row]
        specs += [
            whole(ln1_gain),
            whole(ln1_bias),
            of_layer(w_qkv, layer),
            of_layer(w_attn_out, layer),
            whole(ln2_gain),
            whole(ln2_bias),
            of_layer(router_wide, layer),
            col_spec(layer),
            row_spec_of(layer),
        ]
        shapes = [] if first else [shape_of((images, sp, width), F32)]
        shapes += [
            shape_of((images, sp, 3 * width), BF16),
            shape_of((images, HEADS, sp, sp), BF16),
            shape_of((images, sp, width), BF16),
            shape_of((images, sp, width), F32),
            shape_of((images, sp, width), BF16),
            shape_of((images, sp, LANES), F32),
            shape_of((images, sp, LANES), F32),
        ]
        out_specs = [per_image(s.shape) for s in shapes] + slot_specs
        scratch = [pltpu.VMEM((images * WIDE, width + 2 * LANES), BF16)]
        if first:
            scratch.append(pltpu.VMEM((sp, width), F32))
        out = pl.pallas_call(
            partial(
                forward_kernel,
                first=first,
                layer=layer,
                images=images,
                seq=seq,
                experts=experts,
                **dims,
            ),
            grid=(images,),
            in_specs=specs,
            out_specs=out_specs,
            out_shape=shapes + slot_shapes,
            scratch_shapes=scratch,
            compiler_params=params,
            cost_estimate=cost(6e9, 2e7, 1e6),
            name="forward",
        )(*args)
        out = list(out)
        state = tokens if first else out.pop(0)
        return state, out[:7], nested(out[7:])

    act_shape = shape_of((n * cp, hidden), BF16)
    wire_shape = shape_of((cores, xs, zs, rows, width), BF16)

    def run_expert(layer, j, x, g, saved, forward, backward):
        args = [ids] + [x[d][j] for d in range(n)]
        specs = [smem()] + [whole(slot_shape)] * n
        tile_spec = spec((n * cp, tile), lambda h: (0, h))
        if backward:
            args += [g[d][j] for d in range(n)]
            specs += [whole(slot_shape)] * n
            if not forward:
                made, act, slope = saved
                args += list(made) + [act, slope]
                specs += [whole(slot_shape)] * n + [tile_spec] * 2
        args += [w_in, w_out]
        specs += [
            spec((1, 1, width, tile), lambda h: (layer, j, 0, h)),
            spec((1, 1, tile, width), lambda h: (layer, j, h, 0)),
        ]
        shapes = []
        out_specs = []
        scratch = [pltpu.VMEM((n * cp, width), BF16)]
        if forward:
            shapes += [slot_shape] * n
            out_specs += [whole(slot_shape)] * n
            if not backward:
                shapes += [act_shape] * 2
                out_specs += [tile_spec] * 2
            scratch += [pltpu.VMEM((n * cp, width), F32)]
        if backward:
            shapes += [slot_shape] * n + [wire_shape]
            out_specs += [whole(slot_shape)] * n + [whole(wire_shape)]
            scratch += [pltpu.VMEM((n * cp, width), BF16), pltpu.VMEM((n * cp, width), F32)]
        matmuls = (2 if forward else 0) + (4 if backward else 0)
        return list(
            pl.pallas_call(
                partial(
                    expert_kernel,
                    n=n,
                    cp=cp,
                    tiles=tiles,
                    forward=forward,
                    backward=backward,
                    sizes=(zs, xs, cores, rows_in, rows_out),
                ),
                grid=(tiles,),
                in_specs=specs,
                out_specs=out_specs,
                out_shape=shapes,
                scratch_shapes=scratch,
                compiler_params=params,
                cost_estimate=cost(2 * matmuls * n * cp * width * hidden, 6e6, 2e6 if forward else 0),
                name="expert",
            )(*args)
        )

    kept = []
    previous = None
    for layer in range(layers):
        state, cached, rows_sent = run_forward(layer, previous)
        x = send(rows_sent)
        made = [[None] * per for _ in range(n)]
        d_rows = [[None] * per for _ in range(n)]
        saved = []
        wires = []
        for j in range(per):
            if layer < top:
                out = run_expert(layer, j, x, None, None, True, False)
                saved.append((out[:n], out[n], out[n + 1]))
            else:
                out = run_expert(layer, j, x, g_rows, None, True, True)
                wires.append(out[2 * n])
                for d in range(n):
                    d_rows[d][j] = out[n + d]
            for d in range(n):
                made[d][j] = out[d]
        if layer == top:
            d_back = send_back(d_rows)
        back = send_back(made)
        kept.append((state, cached, x, saved))
        previous = (cached[3], cached[6], back)

    middle, gate, back = previous
    block_out = pl.pallas_call(
        partial(out_kernel, seq=seq, **dims),
        grid=(images,),
        in_specs=[per_image(middle.shape), per_image(gate.shape), col_spec(top)] + slot_specs,
        out_specs=per_image(tokens.shape),
        out_shape=shape_of(tokens.shape, F32),
        compiler_params=params,
        cost_estimate=cost(2 * images * sp * n * per * cp * width, 6e6),
        name="block_out",
    )(middle, gate, col, *flat_of(back))

    dense = [None] * layers
    summed = [None] * layers
    grad = cotangent
    for layer in reversed(range(layers)):
        first = layer == 0
        last = layer == top
        state, cached, x, saved = kept[layer]
        if not last:
            d_rows = [[None] * per for _ in range(n)]
            wires = []
            for j in range(per):
                out = run_expert(layer, j, x, g_rows, saved[j], False, True)
                wires.append(out[n])
                for d in range(n):
                    d_rows[d][j] = out[d]
            d_back = send_back(d_rows)
        summed[layer] = [expert_sum(wire, rep_sizes) for wire in wires]
        joined, probs, attended, middle, moe_in, router, gate = cached
        args = [ids, grad, state, joined, probs, attended, middle, moe_in, router, col]
        specs = [smem()] + [per_image(a.shape) for a in args[1:-1]] + [col_spec(layer)]
        args += flat_of(d_back)
        specs += slot_specs
        args += [ln1_gain, ln1_bias, w_qkv, w_attn_out, ln2_gain, router_wide]
        specs += [
            whole(ln1_gain),
            whole(ln1_bias),
            of_layer(w_qkv, layer),
            of_layer(w_attn_out, layer),
            whole(ln2_gain),
            of_layer(router_wide, layer),
        ]
        dense_shape = shape_of((width, 4 * width + LANES), BF16)
        grad_shape = tokens.shape if first else (images, sp, width)
        shapes = [shape_of(grad_shape, F32), dense_shape]
        out_specs = [per_image(grad_shape), whole(dense_shape)]
        scratch = [
            pltpu.VMEM((n, per, cp, LANES), BF16),
            pltpu.VMEM((width, 3 * width), F32),
            pltpu.VMEM((width, width), F32),
            pltpu.VMEM((width, LANES), F32),
            pltpu.VMEM((8, width), F32),
            pltpu.VMEM((LANES, width), F32),
            pltpu.VMEM((sp, 3 * width), BF16),
        ]
        if last:
            scratch.append(pltpu.VMEM((sp, width), F32))
        if first:
            scratch.append(pltpu.VMEM((sp, width), F32))
        else:
            args.append(row)
            specs.append(row_spec_of(layer - 1))
            shapes += slot_shapes
            out_specs += slot_specs
            scratch.append(pltpu.VMEM((images * WIDE, width), BF16))
        out = pl.pallas_call(
            partial(
                backward_kernel,
                first=first,
                last=last,
                layer=layer,
                images=images,
                seq=seq,
                experts=experts,
                **dims,
            ),
            grid=(images,),
            in_specs=specs,
            out_specs=out_specs,
            out_shape=shapes,
            scratch_shapes=scratch,
            compiler_params=params,
            cost_estimate=cost(1.2e10, 3e7, 0),
            name="backward",
        )(*args)
        grad = out[0]
        dense[layer] = out[1]
        if not first:
            g_rows = send(nested(out[2:]))

    stacked = jnp.stack(dense)
    shares = lax.psum_scatter(stacked, "exp", scatter_dimension=1, tiled=True)
    shares = lax.psum(shares, "rep").astype(F32)
    at = 4 * width
    columns = lambda k: shares[:, :, at + experts + k]
    grad_in = []
    grad_out = []
    for layer in range(layers):
        for total in summed[layer]:
            part = total[: tiles * rows_in].reshape(tiles, rows_in, tile)
            grad_in.append(part.transpose(1, 0, 2).reshape(rows_in, hidden))
            grad_out.append(total[tiles * rows_in :])
    grad_in = jnp.stack(grad_in).reshape(layers, per, rows_in, hidden)
    grad_out = jnp.stack(grad_out).reshape(layers, per, rows_out, width)
    return (
        block_out,
        grad,
        columns(0),
        columns(1),
        shares[:, :, 0 : 3 * width],
        shares[:, :, 3 * width : 4 * width],
        columns(2),
        columns(3),
        shares[:, :, at : at + experts],
        grad_in,
        grad_out,
    )


def solution(mesh):
    return jax.shard_map(
        partial(local, n=mesh.shape["exp"], reps=mesh.shape["rep"]),
        mesh=mesh,
        in_specs=(
            P(("rep", "exp"), None, None),
            P(),
            P(),
            P(),
            P(),
            P(),
            P(),
            P(),
            P(None, "exp", None, None),
            P(None, "exp", None, None),
            P(None, ("rep", "exp"), None),
            P(None, ("rep", "exp"), None),
            P(("rep", "exp"), None, None),
        ),
        out_specs=(
            P(("rep", "exp"), None, None),
            P(("rep", "exp"), None, None),
            P(None, "exp"),
            P(None, "exp"),
            P(None, "exp", None),
            P(None, "exp", None),
            P(None, "exp"),
            P(None, "exp"),
            P(None, "exp", None),
            P(None, "exp", "rep", None),
            P(None, "exp", "rep", None),
        ),
        check_vma=False,
    )
```

```python
from functools import partial

import jax
import jax.numpy as jnp
from jax import lax
from jax.experimental import pallas as pl
from jax.experimental.pallas import tpu as pltpu
from jax.sharding import PartitionSpec as P

HEADS = 8
HEAD_DIM = 64
EPSILON = 1e-06
LANES = 128
WIDE = 256
F32 = jnp.float32
BF16 = jnp.bfloat16
VMEM_LIMIT = 60 * 1024 * 1024


def round_up(value, multiple):
    return -(-value // multiple) * multiple


def nn(a, b):
    return lax.dot_general(a, b, (((1,), (0,)), ((), ())), preferred_element_type=F32)


def nt(a, b):
    return lax.dot_general(a, b, (((1,), (1,)), ((), ())), preferred_element_type=F32)


def tn(a, b):
    return lax.dot_general(a, b, (((0,), (0,)), ((), ())), preferred_element_type=F32)


def iota(shape, dim):
    return lax.broadcasted_iota(jnp.int32, shape, dim)


def row_to_col(row, rows):
    shape = (rows, row.shape[1])
    return jnp.sum(jnp.where(iota(shape, 0) == iota(shape, 1), row, 0.0), axis=1, keepdims=True)


def col_to_row(col, lanes):
    shape = (col.shape[0], lanes)
    return jnp.sum(jnp.where(iota(shape, 0) == iota(shape, 1), col, 0.0), axis=0, keepdims=True)


def normalized(values):
    average = jnp.mean(values, axis=-1, keepdims=True)
    centred = values - average
    spread = jnp.mean(centred * centred, axis=-1, keepdims=True)
    factor = lax.rsqrt(spread + EPSILON)
    return centred * factor, factor


def norm_back(grad, gain, xhat, factor):
    scaled = grad * gain
    mean_e = jnp.mean(scaled, axis=-1, keepdims=True)
    mean_x = jnp.mean(scaled * xhat, axis=-1, keepdims=True)
    return factor * (scaled - mean_e - xhat * mean_x)


def gelu_both(x):
    phi = 0.5 + 0.5 * lax.erf(x * 0.7071067811865476)
    raised = jnp.exp2((x * x) * -0.7213475204444817)
    return x * phi, phi + x * raised * 0.3989422804014327


def route_kernel(ids, r_ref, p_ref, row_ref, col_ref, tall, wide, *, n, per, cap, cp, images, seq):
    tokens = images * seq
    bits = (2 * tokens - 1).bit_length()
    my_exp, my_core = ids[0], ids[1]
    key = (r_ref[0] << bits) + p_ref[0]
    tall[...] = jnp.full(tall.shape, -1, jnp.int32)
    tall[0:tokens, 0:2] = key
    flipped = tall[...].T
    lanes = tall.shape[0]
    slots = []
    experts = []
    for k in range(2):
        mine = flipped[k : k + 1, :]
        expert = mine >> bits
        least = expert << bits
        count = jnp.zeros((1, lanes), jnp.int32)
        for other in range(2):
            theirs = key[:, other : other + 1]
            hit = jnp.logical_and(theirs >= least, theirs < mine)
            count = count + jnp.sum(jnp.where(hit, 1, 0), axis=0, keepdims=True)
        group = jnp.zeros((1, lanes), jnp.int32)
        for q in range(1, n):
            group = group + jnp.where(expert >= q * per, 1, 0)
        ahead = (group >> 1) - my_exp
        ahead = jnp.where(ahead < 0, ahead + n // 2, ahead)
        ahead = 2 * ahead + jnp.where((group & 1) == my_core, 0, 1)
        slot = (ahead * per + (expert - group * per)) * cp + count
        kept = count < cap
        slots.append(jnp.where(kept, slot, -1))
        experts.append(jnp.where(kept, expert, -1))
    table = jnp.concatenate(slots + experts + [jnp.full((4, lanes), -1, jnp.int32)], axis=0)
    sp = col_ref.shape[2]
    for i in range(images):
        moved = table if i == 0 else pltpu.roll(table, lanes - seq * i, axis=1)
        piece = moved[:, :WIDE]
        piece = jnp.where(iota(piece.shape, 1) < seq, piece, -1)
        row_ref[0, :, i * WIDE : (i + 1) * WIDE] = piece
        wide[0:8, :] = piece
        col_ref[0, i] = wide[...].T[0:sp, :]


def first_expert(ids, d, n, per):
    side = lax.rem(ids[0] + d // 2, n // 2)
    core = ids[1] if d % 2 == 0 else 1 - ids[1]
    return (2 * side + core) * per


def spread_rows(ids, row_ref, rhs, outs, n, per, cp, width, experts):
    slots0 = row_ref[0, 0:1, :]
    slots1 = row_ref[0, 1:2, :]
    shape = (per * cp, row_ref.shape[2])
    for d in list(range(1, n)) + [0]:
        place = iota(shape, 0) + d * per * cp
        pick = jnp.where(jnp.logical_or(place == slots0, place == slots1), 1.0, 0.0).astype(BF16)
        rows = nn(pick, rhs[...])
        base = first_expert(ids, d, n, per)
        for j in range(per):
            part = rows[j * cp : (j + 1) * cp, :]
            data = part[:, :width]
            if experts:
                both = part[:, width : width + LANES] + part[:, width + LANES :]
                gate = jnp.sum(
                    jnp.where(iota(both.shape, 1) == base + j, both, 0.0), axis=1, keepdims=True
                )
                line = col_to_row(gate, width)
                high = line.astype(BF16).astype(F32)
                where = iota(data.shape, 0)
                data = jnp.where(where == cp - 1, high, data)
                data = jnp.where(where == cp - 2, line - high, data)
            if len(outs[d]) == per:
                outs[d][j][...] = data.astype(BF16)
            else:
                outs[d][0][j * cp : (j + 1) * cp, :] = data.astype(BF16)


def gathered(c0, c1, v0, v1, back, n, per, cp):
    shape = (c0.shape[0], cp)
    place = iota(shape, 1)
    total = None
    for d in range(n):
        for j in range(per):
            base = (d * per + j) * cp
            pick = jnp.where(c0 - base == place, v0, 0.0) + jnp.where(c1 - base == place, v1, 0.0)
            term = nn(pick.astype(BF16), back[d][j][...])
            total = term if total is None else total + term
    return total


def take(it, n, per):
    return [[next(it) for _ in range(per)] for _ in range(n)]


def head_masks():
    lane = iota((1, LANES), 1)
    low = jnp.where(lane < HEAD_DIM, 1.0, 0.0).astype(BF16)
    high = jnp.where(lane < HEAD_DIM, 0.0, 1.0).astype(BF16)
    return low, high


def forward_kernel(*refs, first, layer, n, per, cp, images, seq, experts):
    it = iter(refs)
    ids = next(it)
    if first:
        x_ref = next(it)
    else:
        mid_in, gate_in, col_in = next(it), next(it), next(it)
        back = take(it, n, per)
    g1, b1, wqkv, wo, g2, b2, wr, col, row = (next(it) for _ in range(9))
    if not first:
        state_out = next(it)
    joined_out, probs_out, attended_out, middle_out, moe_out, rp_out, gate_out = (
        next(it) for _ in range(7)
    )
    disp = take(it, n, per)
    rhs = next(it)
    i = pl.program_id(0)
    sp = middle_out.shape[1]
    width = middle_out.shape[2]

    @pl.when(i == 0)
    def _():
        rhs[...] = jnp.zeros(rhs.shape, BF16)

    if first:
        xs = next(it)

        @pl.when(i == 0)
        def _():
            xs[...] = jnp.zeros(xs.shape, F32)

        xs[0:seq, :] = x_ref[0]
        state = xs[...]
    else:
        state = mid_in[0] + gathered(
            col_in[0, 0, :, 0:1],
            col_in[0, 0, :, 1:2],
            gate_in[0, :, 0:1],
            gate_in[0, :, 1:2],
            back,
            n,
            per,
            cp,
        )
        state_out[0] = state
    xhat, _ = normalized(state)
    normed = (xhat * g1[layer : layer + 1, :] + b1[layer : layer + 1, :]).astype(BF16)
    joined = nn(normed, wqkv[0]).astype(BF16)
    joined_out[0] = joined
    masks = head_masks()
    valid = iota((1, sp), 1) < seq
    pieces = []
    for pair in range(HEADS // 2):
        at = pair * LANES
        q = joined[:, at : at + LANES]
        k = joined[:, width + at : width + at + LANES]
        v = joined[:, 2 * width + at : 2 * width + at + LANES]
        mixed = None
        for half in range(2):
            scores = jnp.where(valid, nt(q, k * masks[half]), -1e30)
            top = jnp.max(scores, axis=-1, keepdims=True)
            raised = jnp.exp((scores - top) * HEAD_DIM ** (-0.5))
            total = jnp.sum(raised, axis=-1, keepdims=True)
            probs = (raised * (1.0 / total)).astype(BF16)
            probs_out[0, 2 * pair + half] = probs
            term = nn(probs, v * masks[half])
            mixed = term if mixed is None else mixed + term
        pieces.append(mixed.astype(BF16))
    attended = jnp.concatenate(pieces, axis=1)
    attended_out[0] = attended
    middle = state + nn(attended, wo[0])
    middle_out[0] = middle
    xhat, _ = normalized(middle)
    moe_in = (xhat * g2[layer : layer + 1, :] + b2[layer : layer + 1, :]).astype(BF16)
    moe_out[0] = moe_in
    logits = nn(moe_in, wr[0])
    lane = iota(logits.shape, 1)
    logits = jnp.where(lane < experts, logits, -1e30)
    raised = jnp.exp(logits - jnp.max(logits, axis=-1, keepdims=True))
    router = raised * (1.0 / jnp.sum(raised, axis=-1, keepdims=True))
    rp_out[0] = router
    gates = []
    for k in range(2):
        chosen = col[0, 0, :, 2 + k : 3 + k]
        gates.append(jnp.sum(jnp.where(lane == chosen, router, 0.0), axis=1, keepdims=True))
    gate_out[0] = jnp.where(lane == 0, gates[0], jnp.where(lane == 1, gates[1], 0.0))
    high = router.astype(BF16)
    low = (router - high.astype(F32)).astype(BF16)
    at = pl.multiple_of(i * WIDE, WIDE)
    rhs[pl.ds(at, sp), 0:width] = moe_in
    rhs[pl.ds(at, sp), width : width + LANES] = high
    rhs[pl.ds(at, sp), width + LANES : width + 2 * LANES] = low

    @pl.when(i == images - 1)
    def _():
        spread_rows(ids, row, rhs, disp, n, per, cp, width, experts)


def cotangent_kernel(*refs, n, per, cp, images, seq):
    it = iter(refs)
    ids, g_ref, row = next(it), next(it), next(it)
    outs = take(it, n, 1)
    rhs = next(it)
    rhs[...] = jnp.zeros(rhs.shape, BF16)
    for i in range(images):
        rhs[i * WIDE : i * WIDE + seq, :] = g_ref[i].astype(BF16)
    spread_rows(ids, row, rhs, outs, n, per, cp, rhs.shape[1], 0)


def out_kernel(*refs, n, per, cp, seq):
    it = iter(refs)
    mid, gate, col = next(it), next(it), next(it)
    joint = take(it, n, 1)
    back = [[part[0].at[pl.ds(j * cp, cp)] for j in range(per)] for part in joint]
    out = next(it)
    state = mid[0] + gathered(
        col[0, 0, :, 0:1], col[0, 0, :, 1:2], gate[0, :, 0:1], gate[0, :, 1:2], back, n, per, cp
    )
    out[0] = state[0:seq, :]


def slot_gates(rows, cp):
    tail = rows[cp - 16 : cp, 0:WIDE].astype(F32)
    line = jnp.sum(jnp.where(iota(tail.shape, 0) >= 14, tail, 0.0), axis=0, keepdims=True)
    return row_to_col(line, cp)


def expert_kernel(*refs, n, cp, tiles, produce, backward, joined):
    it = iter(refs)
    next(it)
    xs = [next(it) for _ in range(n)]
    if backward:
        gs = [next(it) for _ in range(n)]
        if not produce:
            made = [next(it) for _ in range(n)]
    earlier = [[next(it) for _ in range(n)] for _ in range(joined)]
    w_in, w_out = next(it), next(it)
    if produce:
        prod = [next(it) for _ in range(n)]
    if backward:
        dx = [next(it) for _ in range(n)]
        act_s, dpre_s, dprod_out = next(it), next(it), next(it)
    xcat = next(it)
    if not backward:
        act_s = next(it)
    if produce:
        acc_p = next(it)
    if backward:
        dprod, acc_d = next(it), next(it)
    h = pl.program_id(0)
    width = xcat.shape[1]

    @pl.when(h == 0)
    def _():
        for d in range(n):
            xcat[d * cp : (d + 1) * cp, :] = xs[d][...]
            if backward:
                gate = slot_gates(xs[d], cp)
                part = (gate * gs[d][...].astype(F32)).astype(BF16)
                dprod[d * cp : (d + 1) * cp, :] = part
                dprod_out[d * cp : (d + 1) * cp, :] = part
        if produce:
            acc_p[...] = jnp.zeros(acc_p.shape, F32)
        if backward:
            acc_d[...] = jnp.zeros(acc_d.shape, F32)

    step = 16
    pre = nn(xcat[...], w_in[0, 0])
    if backward:
        d_act = nt(dprod[...], w_out[0, 0])
    for r in range(0, n * cp, step):
        rows = slice(r, r + step)
        value, slope = gelu_both(pre[rows, :])
        act_s[rows, :] = value.astype(BF16)
        if backward:
            dpre_s[rows, :] = (d_act[rows, :] * slope).astype(BF16)
    if produce:
        acc_p[...] += nn(act_s[...], w_out[0, 0])
    if backward:
        acc_d[...] += nt(dpre_s[...], w_in[0, 0])

    @pl.when(h == tiles - 1)
    def _():
        for d in range(n):
            rows = pl.ds(d * cp, cp)
            if produce:
                result = acc_p[rows, :].astype(BF16)
                prod[d][joined * cp :, :] = result
                for k in range(joined):
                    prod[d][k * cp : (k + 1) * cp, :] = earlier[k][d][...]
            if backward:
                if not produce:
                    result = made[d][...]
                d_gate = jnp.sum(
                    result.astype(F32) * gs[d][...].astype(F32), axis=1, keepdims=True
                )
                line = col_to_row(d_gate, width)
                data = acc_d[rows, :]
                dx[d][...] = jnp.where(iota(data.shape, 0) == cp - 1, line, data).astype(BF16)


def place_of(index, order):
    return sum(((index >> bit) & 1) << (len(order) - 1 - k) for k, bit in enumerate(order))


def weight_kernel(*refs, n, cp, tiles, wire, follows):
    it = iter(refs)
    ids = next(it)
    xs = [next(it) for _ in range(n)]
    act, dpre, dprod = next(it), next(it), next(it)
    if follows:
        next(it)
    reps, rows_in, rows_out, order_out, order_in, out_at, in_at, whole_at = wire
    wire_refs = [next(it) for _ in range(4 if whole_at is None else 1)]
    xcat, wires, sems = next(it), [next(it), next(it)], next(it)
    h = pl.program_id(0)
    mine_out, mine_in = ids[out_at], ids[in_at]

    @pl.when(h == 0)
    def _():
        for d in range(n):
            xcat[d * cp : (d + 1) * cp, :] = xs[d][...]

    grad_out = tn(act[...], dprod[...]).astype(BF16)
    for q in range(reps // tiles):
        spot = place_of(h * (reps // tiles) + q, order_out) ^ mine_out
        wires[0][spot] = grad_out[q * rows_out : (q + 1) * rows_out, :]
    grad_in = tn(xcat[...], dpre[...]).astype(BF16)
    line = pl.multiple_of(h * rows_in, rows_in)
    for q in range(reps):
        spot = place_of(q, order_in) ^ mine_in
        wires[1][spot, pl.ds(line, rows_in), :] = grad_in[q * rows_in : (q + 1) * rows_in, :]

    @pl.when(h == tiles - 1)
    def _():
        copies = []
        half = wires[0].shape[0] // 2
        rows = wires[0].shape[1]
        for k in range(2):
            for part in range(2):
                if whole_at is None:
                    target = wire_refs[2 * k + part]
                else:
                    place = pl.ds((2 * whole_at + k) * rows, rows)
                    target = wire_refs[0].at[pl.ds(part * half, half), place]
                copies.append(
                    pltpu.make_async_copy(
                        wires[k].at[pl.ds(part * half, half)], target, sems.at[2 * k + part]
                    )
                )
        for copy in copies:
            copy.start()
        for copy in copies:
            copy.wait()


def halve_kernel(*refs, count):
    for k in range(count):
        mine, got, keep, rest = refs[k], refs[count + k], refs[2 * count + k], refs[3 * count + k]
        half = keep.shape[0]
        keep[...] = (mine[:half].astype(F32) + got[:half].astype(F32)).astype(BF16)
        rest[...] = (mine[half:].astype(F32) + got[half:].astype(F32)).astype(BF16)


def finish_kernel(*refs, layers, pairs, tiles, rows_in):
    it = iter(refs)
    ids = next(it)
    parts = [[(next(it), next(it)) for _ in range(2)] for _ in range(pairs)]
    joint = next(it), next(it)
    grad_in, grad_out = next(it), next(it)
    rows, tile = grad_out.shape[2:]
    for layer in range(layers):
        for j in range(pairs):
            for side in range(2):
                core = ids[1] if side == 0 else 1 - ids[1]
                expert = core * pairs + j
                if layer == 0:
                    one, two = parts[j][0][side].at[0], parts[j][1][side].at[0]
                else:
                    one = joint[side].at[0, pl.ds(2 * j * rows, rows)]
                    two = joint[side].at[0, pl.ds((2 * j + 1) * rows, rows)]
                grad_out[layer, expert] = one[...].astype(F32)
                for h in range(tiles):
                    grad_in[layer, expert, :, h * tile : (h + 1) * tile] = two[
                        h * rows_in : (h + 1) * rows_in, :
                    ].astype(F32)


def add_kernel(*refs):
    a, b, outs = refs[0], refs[1], refs[2:]
    for k, out in enumerate(outs):
        one, two = (a, b) if len(a.shape) == 2 else (a.at[k], b.at[k])
        out[...] = (one[...].astype(F32) + two[...].astype(F32)).astype(BF16)


def dense_kernel(*refs, layers, width, experts):
    it = iter(refs)
    ids = next(it)
    parts = [next(it), next(it)]
    qkv, out, router = next(it), next(it), next(it)
    norms = [next(it) for _ in range(4)]
    tall = next(it)
    half = parts[0].shape[1]
    for layer in range(layers):
        for side in range(2):
            core = ids[1] if side == 0 else 1 - ids[1]
            rows = pl.ds(pl.multiple_of(core * half, half), half)
            part = parts[side].at[layer]
            qkv[layer, rows, :] = part[:, 0 : 3 * width].astype(F32)
            out[layer, rows, :] = part[:, 3 * width : 4 * width].astype(F32)
            small = part[:, 4 * width :].astype(F32)
            router[layer, rows, :] = small[:, 0:experts]
            tall[rows, :] = small
        flipped = tall[...].T
        for k in range(4):
            norms[k][layer : layer + 1, :] = flipped[experts + k : experts + k + 1, 0 : 2 * half]


def backward_kernel(*refs, first, last, layer, n, per, cp, images, seq, experts):
    it = iter(refs)
    ids, g_ref, s_ref = next(it), next(it), next(it)
    joined_in, probs_in, attended_in, middle_in, moe_in, rp_in, col = (next(it) for _ in range(7))
    back = take(it, n, per)
    g1, b1, wqkv, wo, g2, wr = (next(it) for _ in range(6))
    if not first:
        row = next(it)
    g_out = next(it)
    dense = [next(it), next(it)]
    if not first:
        outs = take(it, n, per)
    d_cols, a_qkv, a_out, a_router, stats, flip, d_join = (next(it) for _ in range(7))
    if last:
        g_pad = next(it)
    if first:
        s_pad = next(it)
    else:
        rhs = next(it)
    i = pl.program_id(0)
    sp = middle_in.shape[1]
    width = middle_in.shape[2]

    @pl.when(i == 0)
    def _():
        a_qkv[...] = jnp.zeros(a_qkv.shape, F32)
        a_out[...] = jnp.zeros(a_out.shape, F32)
        a_router[...] = jnp.zeros(a_router.shape, F32)
        stats[...] = jnp.zeros(stats.shape, F32)
        flip[...] = jnp.zeros(flip.shape, F32)
        if last:
            g_pad[...] = jnp.zeros(g_pad.shape, F32)
        if first:
            s_pad[...] = jnp.zeros(s_pad.shape, F32)
        else:
            rhs[...] = jnp.zeros(rhs.shape, BF16)
        for d in range(n):
            base = first_expert(ids, d, n, per)
            for j in range(per):
                tail = back[d][j][cp - 16 : cp, 0:WIDE].astype(F32)
                line = jnp.sum(jnp.where(iota(tail.shape, 0) == 15, tail, 0.0), axis=0, keepdims=True)
                column = row_to_col(line, cp)
                d_cols[d, j] = jnp.where(iota((cp, LANES), 1) == base + j, column, 0.0).astype(BF16)

    if last:
        g_pad[0:seq, :] = g_ref[0]
        g = g_pad[...]
    else:
        g = g_ref[0]
    if first:
        s_pad[0:seq, :] = s_ref[0]
        state = s_pad[...]
    else:
        state = s_ref[0]

    c0 = col[0, 0, :, 0:1]
    c1 = col[0, 0, :, 1:2]
    place = iota((sp, cp), 1)
    d_moe = None
    d_rp = None
    for d in range(n):
        for j in range(per):
            base = (d * per + j) * cp
            pick = jnp.where(jnp.logical_or(c0 - base == place, c1 - base == place), 1.0, 0.0)
            pick = pick.astype(BF16)
            term = nn(pick, back[d][j][...])
            small = nn(pick, d_cols[d, j])
            d_moe = term if d_moe is None else d_moe + term
            d_rp = small if d_rp is None else d_rp + small
    router = rp_in[0]
    d_logits = router * (d_rp - jnp.sum(d_rp * router, axis=-1, keepdims=True))
    d_logits = d_logits.astype(BF16)
    a_router[...] += tn(moe_in[0], d_logits)
    d_moe = d_moe + nt(d_logits, wr[0])
    xhat, factor = normalized(middle_in[0])
    stats[2:3, :] += jnp.sum(d_moe * xhat, axis=0, keepdims=True)
    stats[3:4, :] += jnp.sum(d_moe, axis=0, keepdims=True)
    d_middle = g + norm_back(d_moe, g2[layer : layer + 1, :], xhat, factor)
    d_branch = d_middle.astype(BF16)
    a_out[...] += tn(attended_in[0], d_branch)
    d_att = nt(d_branch, wo[0]).astype(BF16)
    masks = head_masks()
    scale = HEAD_DIM ** (-0.5)
    for pair in range(HEADS // 2):
        at = pair * LANES
        q = joined_in[0, :, at : at + LANES]
        k = joined_in[0, :, width + at : width + at + LANES]
        v = joined_in[0, :, 2 * width + at : 2 * width + at + LANES]
        do = d_att[:, at : at + LANES]
        dq = dk = dv = None
        for half in range(2):
            low = probs_in[0, 2 * pair + half]
            probs = low.astype(F32)
            dp = nt(do, v * masks[half])
            ds = (probs * (dp - jnp.sum(dp * probs, axis=-1, keepdims=True))).astype(BF16)
            terms = (
                nn(ds, k * masks[half]),
                tn(ds, q * masks[half]),
                tn(low, do * masks[half]),
            )
            if half == 0:
                dq, dk, dv = terms
            else:
                dq, dk, dv = dq + terms[0], dk + terms[1], dv + terms[2]
        d_join[:, at : at + LANES] = (dq * scale).astype(BF16)
        d_join[:, width + at : width + at + LANES] = (dk * scale).astype(BF16)
        d_join[:, 2 * width + at : 2 * width + at + LANES] = dv.astype(BF16)
    xhat, factor = normalized(state)
    normed = (xhat * g1[layer : layer + 1, :] + b1[layer : layer + 1, :]).astype(BF16)
    a_qkv[...] += tn(normed, d_join[...])
    d_normed = nt(d_join[...], wqkv[0])
    stats[0:1, :] += jnp.sum(d_normed * xhat, axis=0, keepdims=True)
    stats[1:2, :] += jnp.sum(d_normed, axis=0, keepdims=True)
    result = d_middle + norm_back(d_normed, g1[layer : layer + 1, :], xhat, factor)
    if first:
        g_out[0] = result[0:seq, :]
    else:
        g_out[0] = result
        rhs[pl.ds(pl.multiple_of(i * WIDE, WIDE), sp), :] = result.astype(BF16)

    @pl.when(i == images - 1)
    def _():
        if not first:
            spread_rows(ids, row, rhs, outs, n, per, cp, width, 0)
        flip[experts : experts + 8, :] = stats[...]
        a_router[...] += flip[...].T
        half = dense[0].shape[1]
        for core in range(2):

            @pl.when(ids[1] == core)
            def _():
                for side in range(n // 2):
                    spot = ids[0] ^ side
                    for target, c in ((dense[0], core), (dense[1], 1 - core)):
                        rows = slice((2 * side + c) * half, (2 * side + c + 1) * half)
                        target[spot, :, 0 : 3 * width] = a_qkv[rows, :].astype(BF16)
                        target[spot, :, 3 * width : 4 * width] = a_out[rows, :].astype(BF16)
                        target[spot, :, 4 * width :] = a_router[rows, :].astype(BF16)


def spec(shape, index):
    return pl.BlockSpec(shape, index)


def whole(array):
    zeros = (0,) * len(array.shape)
    return pl.BlockSpec(tuple(array.shape), lambda *_: zeros)


def smem():
    return pl.BlockSpec(memory_space=pltpu.SMEM)


def shape_of(shape, dtype):
    return jax.ShapeDtypeStruct(tuple(shape), dtype)


def cost(flops, moved, special=0):
    return pl.CostEstimate(flops=int(flops), bytes_accessed=int(moved), transcendentals=int(special))


def per_image(shape):
    rest = (0,) * (len(shape) - 1)
    return pl.BlockSpec((1,) + tuple(shape[1:]), lambda i: (i,) + rest)


def of_layer(array, layer):
    rest = (0,) * (len(array.shape) - 1)
    return pl.BlockSpec((1,) + tuple(array.shape[1:]), lambda *_: (layer,) + rest)


def swap(values, axis, distance, total):
    return lax.ppermute(values, axis, [(r, r ^ distance) for r in range(total)])


class Line:
    def __init__(self):
        self.last = None

    def __call__(
        self, kernel, args, in_specs, out_specs, out_shape, grid, scratch=(), price=None, name=None, ahead=0, carry=(), after=(), aliases=None
    ):
        anywhere = pl.BlockSpec(memory_space=pl.ANY)
        args, in_specs = list(args), list(in_specs)
        out_specs, out_shape = list(out_specs), list(out_shape)
        spot, spot_out = len(args), len(args) + len(out_specs)
        aliases = dict(aliases or {})
        aliases.update({spot + k: len(out_specs) + k for k in range(len(carry))})
        known = self.last is None or any(self.last is x for x in list(args) + list(carry))
        unread = list(carry) + list(after) + ([] if known else [self.last])
        args += unread
        in_specs += [anywhere] * len(unread)
        out_specs += [anywhere] * len(carry)
        out_shape += [shape_of(c.shape, c.dtype) for c in carry]

        def body(*refs):
            outs_at = spot + len(unread)
            outs_end = outs_at + spot_out - spot
            kernel(*refs[:spot], *refs[outs_at:outs_end], *refs[outs_end + len(carry) :])

        out = pl.pallas_call(
            body,
            grid_spec=pltpu.PrefetchScalarGridSpec(
                num_scalar_prefetch=ahead,
                grid=grid,
                in_specs=in_specs,
                out_specs=list(out_specs),
                scratch_shapes=list(scratch),
            ),
            out_shape=list(out_shape),
            input_output_aliases=aliases,
            compiler_params=pltpu.CompilerParams(
                vmem_limit_bytes=VMEM_LIMIT, dimension_semantics=("arbitrary",)
            ),
            cost_estimate=price,
            name=name,
        )(*args)
        out = list(out)
        self.last = out[0]
        return out


def halve(line, mine, got, carry=(), after=()):
    count = len(mine)
    parts = [shape_of((m.shape[0] // 2,) + tuple(m.shape[1:]), BF16) for m in mine]
    size = sum(m.size for m in mine)
    out = line(
        partial(halve_kernel, count=count),
        list(mine) + list(got),
        [whole(m) for m in list(mine) + list(got)],
        [whole(p) for p in parts + parts],
        parts + parts,
        (1,),
        price=cost(size, 6 * size),
        name="halve",
        carry=carry,
        after=after,
    )
    return out[:count], out[count : 2 * count], out[2 * count :]


def add(line, a, b):
    count = a.shape[0] if len(a.shape) == 3 else 1
    part = shape_of(a.shape[-2:], BF16)
    out = line(
        add_kernel,
        [a, b],
        [whole(a), whole(b)],
        [whole(part)] * count,
        [part] * count,
        (1,),
        price=cost(a.size, 6 * a.size),
        name="add",
    )
    return out if len(a.shape) == 3 else out[0]


def local(
    tokens,
    ln1_gain,
    ln1_bias,
    w_qkv,
    w_attn_out,
    ln2_gain,
    ln2_bias,
    w_router,
    w_in,
    w_out,
    routes,
    priority,
    cotangent,
    n_exp,
    reps,
):
    images, seq, width = tokens.shape
    tok_count = images * seq
    layers, local_experts, _, hidden = w_in.shape
    experts = n_exp * local_experts
    zs, cores = 4, 2
    xs = reps // (zs * cores)
    n = n_exp * cores
    per = local_experts // cores
    cap = 2 * tok_count // experts
    cp = round_up(cap + 2, 16)
    sp = round_up(seq, 16)
    tiles = zs
    tile = hidden // tiles
    rows_in = width // reps
    rows_out = hidden // reps
    bits = reps.bit_length() - 1
    x_bits = list(range(1, bits - 2))
    z_bits = [bits - 2, bits - 1]
    me_rep = lax.axis_index("rep")
    me_exp = lax.axis_index("exp")
    core = me_rep % cores
    x_first = x_bits + z_bits + [0]
    z_first = z_bits[:1] + x_bits + z_bits[1:] + [0]
    ids = jnp.stack(
        [me_exp, core, place_of(me_rep, x_first), place_of(me_rep, z_first)]
    ).astype(jnp.int32)
    router_wide = jnp.pad(w_router, ((0, 0), (0, 0), (0, LANES - experts)))
    dims = dict(n=n, per=per, cp=cp)

    lanes = round_up(tok_count, LANES)
    line = Line()
    row, col = line(
        partial(route_kernel, cap=cap, images=images, seq=seq, **dims),
        [ids, routes, priority],
        [smem()] + [spec((1, tok_count, 2), lambda l: (l, 0, 0))] * 2,
        [
            spec((1, 8, images * WIDE), lambda l: (l, 0, 0)),
            spec((1, images, sp, LANES), lambda l: (l, 0, 0, 0)),
        ],
        [
            shape_of((layers, 8, images * WIDE), jnp.int32),
            shape_of((layers, images, sp, LANES), jnp.int32),
        ],
        (layers,),
        [pltpu.VMEM((lanes, LANES), jnp.int32), pltpu.VMEM((LANES, WIDE), jnp.int32)],
        cost(4e7, 1e6),
        "route",
    )

    slot_shape = shape_of((cp, width), BF16)
    slot_shapes = [slot_shape] * (n * per)
    slot_specs = [whole(slot_shape)] * (n * per)
    joint_shapes = [shape_of((per * cp, width), BF16)] * n
    joint_specs = [whole(joint_shapes[0])] * n

    def nested(flat):
        return [list(flat[d * per : (d + 1) * per]) for d in range(n)]

    def flat_of(lists):
        return [part for group in lists for part in group]

    axes = ("rep", "exp")

    def shifted(d, back):
        pairs = []
        for r in range(reps):
            for y in range(n_exp):
                there = (r ^ (d % 2)) * n_exp + (y + d // 2) % n_exp
                here = r * n_exp + y
                pairs.append((there, here) if back else (here, there))
        return pairs

    def move(lists, back):
        result = [lists[0]]
        for d in range(1, n):
            result.append([lax.ppermute(part, axes, shifted(d, back)) for part in lists[d]])
        return result

    def go_back(part, d):
        return part if d == 0 else lax.ppermute(part, axes, shifted(d, True))

    def send(lists):
        return move(lists, False)

    def send_back(lists):
        return move(lists, True)

    def col_spec(layer):
        return spec((1, 1, sp, LANES), lambda i: (layer, i, 0, 0))

    row_spec_of = lambda layer: spec((1, 8, images * WIDE), lambda *_: (layer, 0, 0))

    top = layers - 1

    def spread_cotangent():
        return [
            [part]
            for part in line(
                partial(cotangent_kernel, images=images, seq=seq, **dims),
                [ids, cotangent, row],
                [smem(), whole(cotangent), row_spec_of(top)],
                joint_specs,
                joint_shapes,
                (1,),
                [pltpu.VMEM((images * WIDE, width), BF16)],
                cost(2 * n * per * cp * images * WIDE * width, 4e6),
                "spread_cotangent",
            )
        ]

    def run_forward(layer, previous):
        first = layer == 0
        args = [ids]
        specs = [smem()]
        if first:
            args += [tokens]
            specs += [per_image(tokens.shape)]
        else:
            middle, gate, back = previous
            args += [middle, gate, col] + flat_of(back)
            specs += [per_image(middle.shape), per_image(gate.shape), col_spec(layer - 1)] + slot_specs
        args += [ln1_gain, ln1_bias, w_qkv, w_attn_out, ln2_gain, ln2_bias, router_wide, col, row]
        specs += [
            whole(ln1_gain),
            whole(ln1_bias),
            of_layer(w_qkv, layer),
            of_layer(w_attn_out, layer),
            whole(ln2_gain),
            whole(ln2_bias),
            of_layer(router_wide, layer),
            col_spec(layer),
            row_spec_of(layer),
        ]
        shapes = [] if first else [shape_of((images, sp, width), F32)]
        shapes += [
            shape_of((images, sp, 3 * width), BF16),
            shape_of((images, HEADS, sp, sp), BF16),
            shape_of((images, sp, width), BF16),
            shape_of((images, sp, width), F32),
            shape_of((images, sp, width), BF16),
            shape_of((images, sp, LANES), F32),
            shape_of((images, sp, LANES), F32),
        ]
        out_specs = [per_image(s.shape) for s in shapes] + slot_specs
        scratch = [pltpu.VMEM((images * WIDE, width + 2 * LANES), BF16)]
        if first:
            scratch.append(pltpu.VMEM((sp, width), F32))
        out = line(
            partial(
                forward_kernel,
                first=first,
                layer=layer,
                images=images,
                seq=seq,
                experts=experts,
                **dims,
            ),
            args,
            specs,
            out_specs,
            shapes + slot_shapes,
            (images,),
            scratch,
            cost(6e9, 2e7, 1e6),
            "forward",
        )
        state = tokens if first else out.pop(0)
        return state, out[:7], nested(out[7:])

    any_spec = pl.BlockSpec(memory_space=pl.ANY)

    def rows_of(lists, j, args, specs):
        for d in range(n):
            array = lists[d][j] if len(lists[d]) > 1 else lists[d][0]
            at = 0 if len(lists[d]) > 1 else j
            args.append(array)
            specs.append(spec((cp, width), lambda *_, at=at: (at, 0)))

    act_shape = shape_of((n * cp, hidden), BF16)
    act_spec = spec((n * cp, tile), lambda h, *_: (0, h))
    cat_shape = shape_of((n * cp, width), BF16)

    def run_expert(layer, j, x, g, made, produce, backward, earlier=()):
        args, specs = [ids], []
        rows_of(x, j, args, specs)
        if backward:
            rows_of(g, j, args, specs)
            if not produce:
                rows_of(made, j, args, specs)
        for parts in earlier:
            args += parts
            specs += [whole(slot_shape)] * n
        args += [w_in, w_out]
        specs += [
            spec((1, 1, width, tile), lambda h, who: (layer, who[1] * per + j, 0, h)),
            spec((1, 1, tile, width), lambda h, who: (layer, who[1] * per + j, h, 0)),
        ]
        shapes = []
        out_specs = []
        scratch = [pltpu.VMEM((n * cp, width), BF16)]
        if not backward:
            scratch.append(pltpu.VMEM((n * cp, tile), BF16))
        if produce:
            made_shape = shape_of(((1 + len(earlier)) * cp, width), BF16)
            shapes += [made_shape] * n
            out_specs += [whole(made_shape)] * n
            scratch += [pltpu.VMEM((n * cp, width), F32)]
        if backward:
            shapes += [slot_shape] * n + [act_shape] * 2 + [cat_shape]
            out_specs += [whole(slot_shape)] * n + [act_spec] * 2 + [whole(cat_shape)]
            scratch += [pltpu.VMEM((n * cp, width), BF16), pltpu.VMEM((n * cp, width), F32)]
        matmuls = (2 if produce else 1) + (2 if backward else 0)
        out = line(
            partial(
                expert_kernel,
                n=n,
                cp=cp,
                tiles=tiles,
                produce=produce,
                backward=backward,
                joined=len(earlier),
            ),
            args,
            specs,
            out_specs,
            shapes,
            (tiles,),
            scratch,
            cost(2 * matmuls * n * cp * width * hidden, 6e6, 2e6),
            "expert",
            1,
        )
        if backward:
            return out[:-3], out[-3:]
        return out, None

    def run_weights(j, x, saved, joint=False, before=None, carry=(), after=()):
        args, specs = [ids], []
        rows_of(x, j, args, specs)
        args += saved
        specs += [act_spec] * 2 + [whole(cat_shape)]
        aliases = {}
        if before is not None:
            aliases = {len(args): 0}
            args.append(before)
            specs.append(any_spec)
        order_in = z_first if j == 0 else x_first
        chunk_out = (reps, rows_out, width)
        chunk_in = (reps, tiles * rows_in, tile)
        if joint:
            natural = list(range(bits - 1, -1, -1))
            wire = (reps, rows_in, rows_out, natural, natural, 1, 1, j)
            shapes = [shape_of((reps, 2 * per * rows_out, width), BF16)]
        else:
            wire = (reps, rows_in, rows_out, x_first, order_in, 2, 3 if j == 0 else 2, None)
            shapes = [shape_of((c[0] // 2,) + c[1:], BF16) for c in (chunk_out,) * 2 + (chunk_in,) * 2]
        out = line(
            partial(
                weight_kernel, n=n, cp=cp, tiles=tiles, wire=wire, follows=before is not None
            ),
            args,
            specs,
            [any_spec] * len(shapes),
            shapes,
            (tiles,),
            [
                pltpu.VMEM((n * cp, width), BF16),
                pltpu.VMEM(chunk_out, BF16),
                pltpu.VMEM(chunk_in, BF16),
                pltpu.SemaphoreType.DMA((4,)),
            ],
            cost(4 * n * cp * width * hidden, 6e6, 0),
            "weights",
            1,
            carry,
            after,
            aliases,
        )
        if joint:
            return out[0], out[1:]
        chunks = [
            dict(mine=out[0], other=out[1], order=x_first, at=0),
            dict(mine=out[2], other=out[3], order=order_in, at=0),
        ]
        return chunks, out[4:]

    def dense_steps(mine, other, result):
        parts = add(line, mine, swap(other, "rep", 1, reps))
        yield
        total = parts[0]
        for side in range(1, n_exp):
            total = add(line, total, swap(parts[side], "exp", side, n_exp))
            yield
        result.append(total)
        while True:
            yield

    def dense_over_chips(totals):
        chips = reps // cores
        parts = jnp.stack([t.reshape(chips, t.shape[0] // chips, t.shape[1]) for t in totals], axis=1)
        parts = lax.all_to_all(
            parts, "rep", split_axis=0, concat_axis=0, axis_index_groups=groups, tiled=True
        )
        share = jnp.sum(parts.astype(F32), axis=0, keepdims=True).astype(BF16)
        parts = lax.all_to_all(
            jnp.broadcast_to(share, parts.shape),
            "rep",
            split_axis=0,
            concat_axis=0,
            axis_index_groups=groups,
            tiled=True,
        )
        full = parts.transpose(1, 0, 2, 3).reshape(layers, totals[0].shape[0], totals[0].shape[1])
        return full, swap(full, "rep", 1, reps)

    def step(process):
        next(process, None)

    def run_out(previous):
        middle, gate, back = previous
        back = flat_of(back)
        return line(
            partial(out_kernel, seq=seq, **dims),
            [middle, gate, col] + back,
            [per_image(middle.shape), per_image(gate.shape), col_spec(top)] + [whole(p) for p in back],
            [per_image(tokens.shape)],
            [shape_of(tokens.shape, F32)],
            (images,),
            (),
            cost(2 * images * sp * n * per * cp * width, 6e6),
            "block_out",
        )[0]

    def run_backward(layer, grad, state, cached, d_back, carry):
        first = layer == 0
        last = layer == top
        joined, probs, attended, middle, moe_in, router, gate = cached
        args = [ids, grad, state, joined, probs, attended, middle, moe_in, router, col]
        specs = [smem()] + [per_image(a.shape) for a in args[1:-1]] + [col_spec(layer)]
        args += flat_of(d_back)
        specs += slot_specs
        args += [ln1_gain, ln1_bias, w_qkv, w_attn_out, ln2_gain, router_wide]
        specs += [
            whole(ln1_gain),
            whole(ln1_bias),
            of_layer(w_qkv, layer),
            of_layer(w_attn_out, layer),
            whole(ln2_gain),
            of_layer(router_wide, layer),
        ]
        dense_shape = shape_of((n_exp, width // n, 4 * width + LANES), BF16)
        grad_shape = tokens.shape if first else (images, sp, width)
        shapes = [shape_of(grad_shape, F32), dense_shape, dense_shape]
        out_specs = [per_image(grad_shape), whole(dense_shape), whole(dense_shape)]
        scratch = [
            pltpu.VMEM((n, per, cp, LANES), BF16),
            pltpu.VMEM((width, 3 * width), F32),
            pltpu.VMEM((width, width), F32),
            pltpu.VMEM((width, LANES), F32),
            pltpu.VMEM((8, width), F32),
            pltpu.VMEM((LANES, width), F32),
            pltpu.VMEM((sp, 3 * width), BF16),
        ]
        if last:
            scratch.append(pltpu.VMEM((sp, width), F32))
        if first:
            scratch.append(pltpu.VMEM((sp, width), F32))
        else:
            args.append(row)
            specs.append(row_spec_of(layer - 1))
            shapes += slot_shapes
            out_specs += slot_specs
            scratch.append(pltpu.VMEM((images * WIDE, width), BF16))
        out = line(
            partial(
                backward_kernel,
                first=first,
                last=last,
                layer=layer,
                images=images,
                seq=seq,
                experts=experts,
                **dims,
            ),
            args,
            specs,
            out_specs,
            shapes,
            (images,),
            scratch,
            cost(1.2e10, 3e7, 0),
            "backward",
            carry=carry,
        )
        count = len(out) - len(carry)
        return out[0], out[1:3], nested(out[3:count]), out[count:]

    def add_up(chunks, carry=(), after=()):
        chunks = [c for c in chunks if c["at"] < bits - 1]
        if not chunks:
            return list(carry)
        got = [swap(c["other"], "rep", 1 << c["order"][c["at"]], reps) for c in chunks]
        keep, rest, carried = halve(line, [c["mine"] for c in chunks], got, carry, after)
        for c, mine, other in zip(chunks, keep, rest):
            c["mine"], c["other"], c["at"] = mine, other, c["at"] + 1
            if c["at"] == bits - 1:
                c["other"] = swap(other, "rep", 1 << c["order"][-1], reps)
        return carried

    def later(chunks, carried):
        for c, other in zip(chunks, carried):
            c["other"] = other

    kept = []
    previous = None
    for layer in range(layers):
        if layer == top:
            g_rows = send(spread_cotangent())
        state, cached, rows_sent = run_forward(layer, previous)
        x = send(rows_sent)
        made = [[] for _ in range(n)]
        if layer < top:
            for j in range(per):
                out, _ = run_expert(layer, j, x, None, None, True, False)
                for d in range(n):
                    made[d].append(out[d])
            previous = (cached[3], cached[6], send_back(made))
        kept.append((state, cached, x, made))

    state, cached, x, _ = kept[top]
    outs, saved = [], []
    d_back = [[] for _ in range(n)]
    for j in range(per):
        earlier = [o[:n] for o in outs] if j == per - 1 else ()
        out, kept_rows = run_expert(top, j, x, g_rows, None, True, True, earlier)
        outs.append(out)
        saved.append(kept_rows)
        for d, part in enumerate(out[n : 2 * n]):
            d_back[d].append(go_back(part, d))
    wire = None
    for j in range(per):
        carry = outs[-1][:n] if j == per - 1 else ()
        wire, made_top = run_weights(j, x, saved[j], True, wire, carry)
    back_top = send_back([[part] for part in made_top])
    groups = [[r for r in range(reps) if r % cores == c] for c in range(cores)]
    share = lax.psum_scatter(
        wire, "rep", scatter_dimension=0, axis_index_groups=groups, tiled=True
    )
    grad, parts, g_rows, _ = run_backward(top, cotangent, state, cached, d_back, ())
    g_rows = send(g_rows)
    dense = [[] for _ in range(layers)]
    flow_top = dense_steps(parts[0], parts[1], dense[top])
    block_out = run_out((cached[3], cached[6], back_top))

    state, cached, x, made = kept[0]
    d_back = [[] for _ in range(n)]
    saved = []
    for j in range(per):
        out, kept_rows = run_expert(0, j, x, g_rows, made, False, True)
        saved.append(kept_rows)
        for k in range(n):
            d_back[k].append(go_back(out[k], k))
        if j == 0:
            step(flow_top)
    sums = []
    for j in range(per):
        new, _ = run_weights(j, x, saved[j])
        sums += new
        if j == 0:
            step(flow_top)
    a, b, c, d = sums
    grad, parts, _, carried = run_backward(0, grad, state, cached, d_back, [d["other"]])
    later([d], carried)
    flow = dense_steps(parts[0], parts[1], dense[0])
    while not dense[top]:
        step(flow_top)
    step(flow)
    add_up([a, b])
    while not dense[0]:
        step(flow)
    halves = list(dense_over_chips([d[0] for d in dense]))
    for group in ((c,), (a,), (d,), (b, c), (a,), (d,), (c, b), (d,)):
        add_up(group)
    for _ in range(bits):
        add_up([a, b, c, d])
    top_mine = share[: share.shape[0] // 2]
    top_other = swap(share[share.shape[0] // 2 :], "rep", 1, reps)
    pieces = [part for k in sums for part in (k["mine"], k["other"])] + [top_mine, top_other]
    in_shape = shape_of((layers, local_experts, rows_in, hidden), F32)
    out_shape = shape_of((layers, local_experts, rows_out, width), F32)
    grad_in, grad_out = line(
        partial(finish_kernel, layers=layers, pairs=per, tiles=tiles, rows_in=rows_in),
        [ids] + pieces,
        [smem()] + [whole(p) for p in pieces],
        [whole(in_shape), whole(out_shape)],
        [in_shape, out_shape],
        (1,),
        (),
        cost(1e6, 6e6),
        "finish",
    )
    rows = width // n_exp
    dense_shapes = [
        shape_of((layers, rows, 3 * width), F32),
        shape_of((layers, rows, width), F32),
        shape_of((layers, rows, experts), F32),
    ] + [shape_of((layers, rows), F32)] * 4
    qkv, attn_out, router, gain1, bias1, gain2, bias2 = line(
        partial(dense_kernel, layers=layers, width=width, experts=experts),
        [ids] + halves,
        [smem()] + [whole(p) for p in halves],
        [whole(s) for s in dense_shapes],
        dense_shapes,
        (1,),
        [pltpu.VMEM((WIDE, LANES), F32)],
        cost(1e6, 6e6),
        "finish_dense",
    )
    return (
        block_out,
        grad,
        gain1,
        bias1,
        qkv,
        attn_out,
        gain2,
        bias2,
        router,
        grad_in,
        grad_out,
    )


def solution(mesh):
    return jax.shard_map(
        partial(local, n_exp=mesh.shape["exp"], reps=mesh.shape["rep"]),
        mesh=mesh,
        in_specs=(
            P(("rep", "exp"), None, None),
            P(),
            P(),
            P(),
            P(),
            P(),
            P(),
            P(),
            P(None, "exp", None, None),
            P(None, "exp", None, None),
            P(None, ("rep", "exp"), None),
            P(None, ("rep", "exp"), None),
            P(("rep", "exp"), None, None),
        ),
        out_specs=(
            P(("rep", "exp"), None, None),
            P(("rep", "exp"), None, None),
            P(None, "exp"),
            P(None, "exp"),
            P(None, "exp", None),
            P(None, "exp", None),
            P(None, "exp"),
            P(None, "exp"),
            P(None, "exp", None),
            P(None, "exp", "rep", None),
            P(None, "exp", "rep", None),
        ),
        check_vma=False,
    )
```

```python
from functools import partial

import jax
import jax.numpy as jnp
from jax import lax
from jax.experimental import pallas as pl
from jax.experimental.pallas import tpu as pltpu
from jax.sharding import PartitionSpec as P

HEADS = 8
HEAD_DIM = 64
EPSILON = 1e-06
LANES = 128
WIDE = 256
F32 = jnp.float32
BF16 = jnp.bfloat16
VMEM_LIMIT = 60 * 1024 * 1024


def round_up(value, multiple):
    return -(-value // multiple) * multiple


def nn(a, b):
    return lax.dot_general(a, b, (((1,), (0,)), ((), ())), preferred_element_type=F32)


def nt(a, b):
    return lax.dot_general(a, b, (((1,), (1,)), ((), ())), preferred_element_type=F32)


def tn(a, b):
    return lax.dot_general(a, b, (((0,), (0,)), ((), ())), preferred_element_type=F32)


def iota(shape, dim):
    return lax.broadcasted_iota(jnp.int32, shape, dim)


def row_to_col(row, rows):
    shape = (rows, row.shape[1])
    return jnp.sum(jnp.where(iota(shape, 0) == iota(shape, 1), row, 0.0), axis=1, keepdims=True)


def col_to_row(col, lanes):
    shape = (col.shape[0], lanes)
    return jnp.sum(jnp.where(iota(shape, 0) == iota(shape, 1), col, 0.0), axis=0, keepdims=True)


def normalized(values):
    average = jnp.mean(values, axis=-1, keepdims=True)
    centred = values - average
    spread = jnp.mean(centred * centred, axis=-1, keepdims=True)
    factor = lax.rsqrt(spread + EPSILON)
    return centred * factor, factor


def norm_back(grad, gain, xhat, factor):
    scaled = grad * gain
    mean_e = jnp.mean(scaled, axis=-1, keepdims=True)
    mean_x = jnp.mean(scaled * xhat, axis=-1, keepdims=True)
    return factor * (scaled - mean_e - xhat * mean_x)


def gelu_both(x):
    phi = 0.5 + 0.5 * lax.erf(x * 0.7071067811865476)
    raised = jnp.exp2((x * x) * -0.7213475204444817)
    return x * phi, phi + x * raised * 0.3989422804014327


def route_kernel(ids, r_ref, p_ref, row_ref, col_ref, tall, wide, *, n, per, cap, cp, images, seq):
    tokens = images * seq
    bits = (2 * tokens - 1).bit_length()
    my_exp, my_core = ids[0], ids[1]
    key = (r_ref[0] << bits) + p_ref[0]
    tall[...] = jnp.full(tall.shape, -1, jnp.int32)
    tall[0:tokens, 0:2] = key
    flipped = tall[...].T
    lanes = tall.shape[0]
    slots = []
    experts = []
    for k in range(2):
        mine = flipped[k : k + 1, :]
        expert = mine >> bits
        least = expert << bits
        count = jnp.zeros((1, lanes), jnp.int32)
        for other in range(2):
            theirs = key[:, other : other + 1]
            hit = jnp.logical_and(theirs >= least, theirs < mine)
            count = count + jnp.sum(jnp.where(hit, 1, 0), axis=0, keepdims=True)
        group = jnp.zeros((1, lanes), jnp.int32)
        for q in range(1, n):
            group = group + jnp.where(expert >= q * per, 1, 0)
        ahead = (group >> 1) - my_exp
        ahead = jnp.where(ahead < 0, ahead + n // 2, ahead)
        ahead = 2 * ahead + jnp.where((group & 1) == my_core, 0, 1)
        slot = (ahead * per + (expert - group * per)) * cp + count
        kept = count < cap
        slots.append(jnp.where(kept, slot, -1))
        experts.append(jnp.where(kept, expert, -1))
    table = jnp.concatenate(slots + experts + [jnp.full((4, lanes), -1, jnp.int32)], axis=0)
    sp = col_ref.shape[2]
    for i in range(images):
        moved = table if i == 0 else pltpu.roll(table, lanes - seq * i, axis=1)
        piece = moved[:, :WIDE]
        piece = jnp.where(iota(piece.shape, 1) < seq, piece, -1)
        row_ref[0, :, i * WIDE : (i + 1) * WIDE] = piece
        wide[0:8, :] = piece
        col_ref[0, i] = wide[...].T[0:sp, :]


def first_expert(ids, d, n, per):
    side = lax.rem(ids[0] + d // 2, n // 2)
    core = ids[1] if d % 2 == 0 else 1 - ids[1]
    return (2 * side + core) * per


def spread_rows(ids, row_ref, rhs, outs, n, per, cp, width, experts):
    slots0 = row_ref[0, 0:1, :]
    slots1 = row_ref[0, 1:2, :]
    shape = (per * cp, row_ref.shape[2])
    for d in list(range(1, n)) + [0]:
        place = iota(shape, 0) + d * per * cp
        pick = jnp.where(jnp.logical_or(place == slots0, place == slots1), 1.0, 0.0).astype(BF16)
        rows = nn(pick, rhs[...])
        base = first_expert(ids, d, n, per)
        for j in range(per):
            part = rows[j * cp : (j + 1) * cp, :]
            data = part[:, :width]
            if experts:
                both = part[:, width : width + LANES] + part[:, width + LANES :]
                gate = jnp.sum(
                    jnp.where(iota(both.shape, 1) == base + j, both, 0.0), axis=1, keepdims=True
                )
                line = col_to_row(gate, width)
                high = line.astype(BF16).astype(F32)
                where = iota(data.shape, 0)
                data = jnp.where(where == cp - 1, high, data)
                data = jnp.where(where == cp - 2, line - high, data)
            if len(outs[d]) == per:
                outs[d][j][...] = data.astype(BF16)
            else:
                outs[d][0][j * cp : (j + 1) * cp, :] = data.astype(BF16)


def gathered(c0, c1, v0, v1, back, n, per, cp):
    shape = (c0.shape[0], cp)
    place = iota(shape, 1)
    total = None
    for d in range(n):
        for j in range(per):
            base = (d * per + j) * cp
            pick = jnp.where(c0 - base == place, v0, 0.0) + jnp.where(c1 - base == place, v1, 0.0)
            term = nn(pick.astype(BF16), back[d][j][...])
            total = term if total is None else total + term
    return total


def take(it, n, per):
    return [[next(it) for _ in range(per)] for _ in range(n)]


def head_masks():
    lane = iota((1, LANES), 1)
    low = jnp.where(lane < HEAD_DIM, 1.0, 0.0).astype(BF16)
    high = jnp.where(lane < HEAD_DIM, 0.0, 1.0).astype(BF16)
    return low, high


def forward_kernel(*refs, first, layer, n, per, cp, images, seq, experts):
    it = iter(refs)
    ids = next(it)
    if first:
        x_ref = next(it)
    else:
        mid_in, gate_in, col_in = next(it), next(it), next(it)
        back = take(it, n, per)
    g1, b1, wqkv, wo, g2, b2, wr, col, row = (next(it) for _ in range(9))
    if not first:
        state_out = next(it)
    joined_out, probs_out, attended_out, middle_out, moe_out, rp_out, gate_out = (
        next(it) for _ in range(7)
    )
    disp = take(it, n, per)
    rhs = next(it)
    i = pl.program_id(0)
    sp = middle_out.shape[1]
    width = middle_out.shape[2]

    @pl.when(i == 0)
    def _():
        rhs[...] = jnp.zeros(rhs.shape, BF16)

    if first:
        xs = next(it)

        @pl.when(i == 0)
        def _():
            xs[...] = jnp.zeros(xs.shape, F32)

        xs[0:seq, :] = x_ref[0]
        state = xs[...]
    else:
        state = mid_in[0] + gathered(
            col_in[0, 0, :, 0:1],
            col_in[0, 0, :, 1:2],
            gate_in[0, :, 0:1],
            gate_in[0, :, 1:2],
            back,
            n,
            per,
            cp,
        )
        state_out[0] = state
    xhat, _ = normalized(state)
    normed = (xhat * g1[layer : layer + 1, :] + b1[layer : layer + 1, :]).astype(BF16)
    joined = nn(normed, wqkv[0]).astype(BF16)
    joined_out[0] = joined
    masks = head_masks()
    valid = iota((1, sp), 1) < seq
    pieces = []
    for pair in range(HEADS // 2):
        at = pair * LANES
        q = joined[:, at : at + LANES]
        k = joined[:, width + at : width + at + LANES]
        v = joined[:, 2 * width + at : 2 * width + at + LANES]
        mixed = None
        for half in range(2):
            scores = jnp.where(valid, nt(q, k * masks[half]), -1e30)
            top = jnp.max(scores, axis=-1, keepdims=True)
            raised = jnp.exp((scores - top) * HEAD_DIM ** (-0.5))
            total = jnp.sum(raised, axis=-1, keepdims=True)
            probs = (raised * (1.0 / total)).astype(BF16)
            probs_out[0, 2 * pair + half] = probs
            term = nn(probs, v * masks[half])
            mixed = term if mixed is None else mixed + term
        pieces.append(mixed.astype(BF16))
    attended = jnp.concatenate(pieces, axis=1)
    attended_out[0] = attended
    middle = state + nn(attended, wo[0])
    middle_out[0] = middle
    xhat, _ = normalized(middle)
    moe_in = (xhat * g2[layer : layer + 1, :] + b2[layer : layer + 1, :]).astype(BF16)
    moe_out[0] = moe_in
    logits = nn(moe_in, wr[0])
    lane = iota(logits.shape, 1)
    logits = jnp.where(lane < experts, logits, -1e30)
    raised = jnp.exp(logits - jnp.max(logits, axis=-1, keepdims=True))
    router = raised * (1.0 / jnp.sum(raised, axis=-1, keepdims=True))
    rp_out[0] = router
    gates = []
    for k in range(2):
        chosen = col[0, 0, :, 2 + k : 3 + k]
        gates.append(jnp.sum(jnp.where(lane == chosen, router, 0.0), axis=1, keepdims=True))
    gate_out[0] = jnp.where(lane == 0, gates[0], jnp.where(lane == 1, gates[1], 0.0))
    high = router.astype(BF16)
    low = (router - high.astype(F32)).astype(BF16)
    at = pl.multiple_of(i * WIDE, WIDE)
    rhs[pl.ds(at, sp), 0:width] = moe_in
    rhs[pl.ds(at, sp), width : width + LANES] = high
    rhs[pl.ds(at, sp), width + LANES : width + 2 * LANES] = low

    @pl.when(i == images - 1)
    def _():
        spread_rows(ids, row, rhs, disp, n, per, cp, width, experts)


def cotangent_kernel(*refs, n, per, cp, images, seq):
    it = iter(refs)
    ids, g_ref, row = next(it), next(it), next(it)
    outs = take(it, n, 1)
    rhs = next(it)
    rhs[...] = jnp.zeros(rhs.shape, BF16)
    for i in range(images):
        rhs[i * WIDE : i * WIDE + seq, :] = g_ref[i].astype(BF16)
    spread_rows(ids, row, rhs, outs, n, per, cp, rhs.shape[1], 0)


def out_kernel(*refs, n, per, cp, seq):
    it = iter(refs)
    mid, gate, col = next(it), next(it), next(it)
    joint = take(it, n, 1)
    back = [[part[0].at[pl.ds(j * cp, cp)] for j in range(per)] for part in joint]
    out = next(it)
    state = mid[0] + gathered(
        col[0, 0, :, 0:1], col[0, 0, :, 1:2], gate[0, :, 0:1], gate[0, :, 1:2], back, n, per, cp
    )
    out[0] = state[0:seq, :]


def slot_gates(rows, cp):
    tail = rows[cp - 16 : cp, 0:WIDE].astype(F32)
    line = jnp.sum(jnp.where(iota(tail.shape, 0) >= 14, tail, 0.0), axis=0, keepdims=True)
    return row_to_col(line, cp)


def expert_kernel(*refs, n, cp, tiles, produce, backward, joined):
    it = iter(refs)
    next(it)
    xs = [next(it) for _ in range(n)]
    if backward:
        gs = [next(it) for _ in range(n)]
        if not produce:
            made = [next(it) for _ in range(n)]
    earlier = [[next(it) for _ in range(n)] for _ in range(joined)]
    w_in, w_out = next(it), next(it)
    if produce:
        prod = [next(it) for _ in range(n)]
    if backward:
        dx = [next(it) for _ in range(n)]
        act_s, dpre_s, dprod_out = next(it), next(it), next(it)
    xcat = next(it)
    if not backward:
        act_s = next(it)
    if produce:
        acc_p = next(it)
    if backward:
        dprod, acc_d = next(it), next(it)
    h = pl.program_id(0)
    width = xcat.shape[1]

    @pl.when(h == 0)
    def _():
        for d in range(n):
            xcat[d * cp : (d + 1) * cp, :] = xs[d][...]
            if backward:
                gate = slot_gates(xs[d], cp)
                part = (gate * gs[d][...].astype(F32)).astype(BF16)
                dprod[d * cp : (d + 1) * cp, :] = part
                dprod_out[d * cp : (d + 1) * cp, :] = part
        if produce:
            acc_p[...] = jnp.zeros(acc_p.shape, F32)
        if backward:
            acc_d[...] = jnp.zeros(acc_d.shape, F32)

    step = 16
    pre = nn(xcat[...], w_in[0, 0])
    if backward:
        d_act = nt(dprod[...], w_out[0, 0])
    for r in range(0, n * cp, step):
        rows = slice(r, r + step)
        value, slope = gelu_both(pre[rows, :])
        act_s[rows, :] = value.astype(BF16)
        if backward:
            dpre_s[rows, :] = (d_act[rows, :] * slope).astype(BF16)
    if produce:
        acc_p[...] += nn(act_s[...], w_out[0, 0])
    if backward:
        acc_d[...] += nt(dpre_s[...], w_in[0, 0])

    @pl.when(h == tiles - 1)
    def _():
        for d in range(n):
            rows = pl.ds(d * cp, cp)
            if produce:
                result = acc_p[rows, :].astype(BF16)
                prod[d][joined * cp :, :] = result
                for k in range(joined):
                    prod[d][k * cp : (k + 1) * cp, :] = earlier[k][d][...]
            if backward:
                if not produce:
                    result = made[d][...]
                d_gate = jnp.sum(
                    result.astype(F32) * gs[d][...].astype(F32), axis=1, keepdims=True
                )
                line = col_to_row(d_gate, width)
                data = acc_d[rows, :]
                dx[d][...] = jnp.where(iota(data.shape, 0) == cp - 1, line, data).astype(BF16)


def weight_kernel(*refs, n, cp, tiles, wire, follows):
    it = iter(refs)
    ids = next(it)
    xs = [next(it) for _ in range(n)]
    act, dpre, dprod = next(it), next(it), next(it)
    if follows:
        next(it)
    reps, rows_in, rows_out, spot_at = wire
    target = next(it)
    xcat, wires, sems = next(it), [next(it), next(it)], next(it)
    h = pl.program_id(0)

    @pl.when(h == 0)
    def _():
        for d in range(n):
            xcat[d * cp : (d + 1) * cp, :] = xs[d][...]

    grad_out = tn(act[...], dprod[...]).astype(BF16)
    for q in range(reps // tiles):
        spot = (h * (reps // tiles) + q) ^ ids[1]
        wires[0][spot] = grad_out[q * rows_out : (q + 1) * rows_out, :]
    grad_in = tn(xcat[...], dpre[...]).astype(BF16)
    line = pl.multiple_of(h * rows_in, rows_in)
    for q in range(reps):
        wires[1][q ^ ids[1], pl.ds(line, rows_in), :] = grad_in[q * rows_in : (q + 1) * rows_in, :]

    @pl.when(h == tiles - 1)
    def _():
        rows = wires[0].shape[1]
        copies = [
            pltpu.make_async_copy(
                wires[k], target.at[:, pl.ds((2 * spot_at + k) * rows, rows)], sems.at[k]
            )
            for k in range(2)
        ]
        for copy in copies:
            copy.start()
        for copy in copies:
            copy.wait()


def finish_kernel(*refs, layers, pairs, tiles, rows_in):
    it = iter(refs)
    ids = next(it)
    parts = [(next(it), next(it)) for _ in range(layers)]
    grad_in, grad_out = next(it), next(it)
    rows, tile = grad_out.shape[2:]
    for layer in range(layers):
        for j in range(pairs):
            for side in range(2):
                core = ids[1] if side == 0 else 1 - ids[1]
                expert = core * pairs + j
                part = parts[layer][side]
                at = 2 * j * rows
                grad_out[layer, expert] = part[0, at : at + rows, :].astype(F32)
                for h in range(tiles):
                    line = at + rows + h * rows_in
                    grad_in[layer, expert, :, h * tile : (h + 1) * tile] = part[
                        0, line : line + rows_in, :
                    ].astype(F32)


def add_kernel(*refs):
    a, b, outs = refs[0], refs[1], refs[2:]
    for k, out in enumerate(outs):
        one, two = (a, b) if len(a.shape) == 2 else (a.at[k], b.at[k])
        out[...] = (one[...].astype(F32) + two[...].astype(F32)).astype(BF16)


def dense_kernel(*refs, layers, width, experts):
    it = iter(refs)
    ids = next(it)
    parts = [next(it), next(it)]
    qkv, out, router = next(it), next(it), next(it)
    norms = [next(it) for _ in range(4)]
    tall = next(it)
    half = parts[0].shape[1]
    for layer in range(layers):
        for side in range(2):
            core = ids[1] if side == 0 else 1 - ids[1]
            rows = pl.ds(pl.multiple_of(core * half, half), half)
            part = parts[side].at[layer]
            qkv[layer, rows, :] = part[:, 0 : 3 * width].astype(F32)
            out[layer, rows, :] = part[:, 3 * width : 4 * width].astype(F32)
            small = part[:, 4 * width :].astype(F32)
            router[layer, rows, :] = small[:, 0:experts]
            tall[rows, :] = small
        flipped = tall[...].T
        for k in range(4):
            norms[k][layer : layer + 1, :] = flipped[experts + k : experts + k + 1, 0 : 2 * half]


def backward_kernel(*refs, first, last, layer, n, per, cp, images, seq, experts):
    it = iter(refs)
    ids, g_ref, s_ref = next(it), next(it), next(it)
    joined_in, probs_in, attended_in, middle_in, moe_in, rp_in, col = (next(it) for _ in range(7))
    back = take(it, n, per)
    g1, b1, wqkv, wo, g2, wr = (next(it) for _ in range(6))
    if not first:
        row = next(it)
    g_out = next(it)
    dense = [next(it), next(it)]
    if not first:
        outs = take(it, n, per)
    d_cols, a_qkv, a_out, a_router, stats, flip, d_join = (next(it) for _ in range(7))
    if last:
        g_pad = next(it)
    if first:
        s_pad = next(it)
    else:
        rhs = next(it)
    i = pl.program_id(0)
    sp = middle_in.shape[1]
    width = middle_in.shape[2]

    @pl.when(i == 0)
    def _():
        a_qkv[...] = jnp.zeros(a_qkv.shape, F32)
        a_out[...] = jnp.zeros(a_out.shape, F32)
        a_router[...] = jnp.zeros(a_router.shape, F32)
        stats[...] = jnp.zeros(stats.shape, F32)
        flip[...] = jnp.zeros(flip.shape, F32)
        if last:
            g_pad[...] = jnp.zeros(g_pad.shape, F32)
        if first:
            s_pad[...] = jnp.zeros(s_pad.shape, F32)
        else:
            rhs[...] = jnp.zeros(rhs.shape, BF16)
        for d in range(n):
            base = first_expert(ids, d, n, per)
            for j in range(per):
                tail = back[d][j][cp - 16 : cp, 0:WIDE].astype(F32)
                line = jnp.sum(jnp.where(iota(tail.shape, 0) == 15, tail, 0.0), axis=0, keepdims=True)
                column = row_to_col(line, cp)
                d_cols[d, j] = jnp.where(iota((cp, LANES), 1) == base + j, column, 0.0).astype(BF16)

    if last:
        g_pad[0:seq, :] = g_ref[0]
        g = g_pad[...]
    else:
        g = g_ref[0]
    if first:
        s_pad[0:seq, :] = s_ref[0]
        state = s_pad[...]
    else:
        state = s_ref[0]

    c0 = col[0, 0, :, 0:1]
    c1 = col[0, 0, :, 1:2]
    place = iota((sp, cp), 1)
    d_moe = None
    d_rp = None
    for d in range(n):
        for j in range(per):
            base = (d * per + j) * cp
            pick = jnp.where(jnp.logical_or(c0 - base == place, c1 - base == place), 1.0, 0.0)
            pick = pick.astype(BF16)
            term = nn(pick, back[d][j][...])
            small = nn(pick, d_cols[d, j])
            d_moe = term if d_moe is None else d_moe + term
            d_rp = small if d_rp is None else d_rp + small
    router = rp_in[0]
    d_logits = router * (d_rp - jnp.sum(d_rp * router, axis=-1, keepdims=True))
    d_logits = d_logits.astype(BF16)
    a_router[...] += tn(moe_in[0], d_logits)
    d_moe = d_moe + nt(d_logits, wr[0])
    xhat, factor = normalized(middle_in[0])
    stats[2:3, :] += jnp.sum(d_moe * xhat, axis=0, keepdims=True)
    stats[3:4, :] += jnp.sum(d_moe, axis=0, keepdims=True)
    d_middle = g + norm_back(d_moe, g2[layer : layer + 1, :], xhat, factor)
    d_branch = d_middle.astype(BF16)
    a_out[...] += tn(attended_in[0], d_branch)
    d_att = nt(d_branch, wo[0]).astype(BF16)
    masks = head_masks()
    scale = HEAD_DIM ** (-0.5)
    for pair in range(HEADS // 2):
        at = pair * LANES
        q = joined_in[0, :, at : at + LANES]
        k = joined_in[0, :, width + at : width + at + LANES]
        v = joined_in[0, :, 2 * width + at : 2 * width + at + LANES]
        do = d_att[:, at : at + LANES]
        dq = dk = dv = None
        for half in range(2):
            low = probs_in[0, 2 * pair + half]
            probs = low.astype(F32)
            dp = nt(do, v * masks[half])
            ds = (probs * (dp - jnp.sum(dp * probs, axis=-1, keepdims=True))).astype(BF16)
            terms = (
                nn(ds, k * masks[half]),
                tn(ds, q * masks[half]),
                tn(low, do * masks[half]),
            )
            if half == 0:
                dq, dk, dv = terms
            else:
                dq, dk, dv = dq + terms[0], dk + terms[1], dv + terms[2]
        d_join[:, at : at + LANES] = (dq * scale).astype(BF16)
        d_join[:, width + at : width + at + LANES] = (dk * scale).astype(BF16)
        d_join[:, 2 * width + at : 2 * width + at + LANES] = dv.astype(BF16)
    xhat, factor = normalized(state)
    normed = (xhat * g1[layer : layer + 1, :] + b1[layer : layer + 1, :]).astype(BF16)
    a_qkv[...] += tn(normed, d_join[...])
    d_normed = nt(d_join[...], wqkv[0])
    stats[0:1, :] += jnp.sum(d_normed * xhat, axis=0, keepdims=True)
    stats[1:2, :] += jnp.sum(d_normed, axis=0, keepdims=True)
    result = d_middle + norm_back(d_normed, g1[layer : layer + 1, :], xhat, factor)
    if first:
        g_out[0] = result[0:seq, :]
    else:
        g_out[0] = result
        rhs[pl.ds(pl.multiple_of(i * WIDE, WIDE), sp), :] = result.astype(BF16)

    @pl.when(i == images - 1)
    def _():
        if not first:
            spread_rows(ids, row, rhs, outs, n, per, cp, width, 0)
        flip[experts : experts + 8, :] = stats[...]
        a_router[...] += flip[...].T
        half = dense[0].shape[1]
        for core in range(2):

            @pl.when(ids[1] == core)
            def _():
                for side in range(n // 2):
                    spot = ids[0] ^ side
                    for target, c in ((dense[0], core), (dense[1], 1 - core)):
                        rows = slice((2 * side + c) * half, (2 * side + c + 1) * half)
                        target[spot, :, 0 : 3 * width] = a_qkv[rows, :].astype(BF16)
                        target[spot, :, 3 * width : 4 * width] = a_out[rows, :].astype(BF16)
                        target[spot, :, 4 * width :] = a_router[rows, :].astype(BF16)


def spec(shape, index):
    return pl.BlockSpec(shape, index)


def whole(array):
    zeros = (0,) * len(array.shape)
    return pl.BlockSpec(tuple(array.shape), lambda *_: zeros)


def smem():
    return pl.BlockSpec(memory_space=pltpu.SMEM)


def shape_of(shape, dtype):
    return jax.ShapeDtypeStruct(tuple(shape), dtype)


def cost(flops, moved, special=0):
    return pl.CostEstimate(flops=int(flops), bytes_accessed=int(moved), transcendentals=int(special))


def per_image(shape):
    rest = (0,) * (len(shape) - 1)
    return pl.BlockSpec((1,) + tuple(shape[1:]), lambda i: (i,) + rest)


def of_layer(array, layer):
    rest = (0,) * (len(array.shape) - 1)
    return pl.BlockSpec((1,) + tuple(array.shape[1:]), lambda *_: (layer,) + rest)


def swap(values, axis, distance, total):
    return lax.ppermute(values, axis, [(r, r ^ distance) for r in range(total)])


class Line:
    def __init__(self):
        self.last = None

    def __call__(
        self, kernel, args, in_specs, out_specs, out_shape, grid, scratch=(), price=None, name=None, ahead=0, carry=(), after=(), aliases=None
    ):
        anywhere = pl.BlockSpec(memory_space=pl.ANY)
        args, in_specs = list(args), list(in_specs)
        out_specs, out_shape = list(out_specs), list(out_shape)
        spot, spot_out = len(args), len(args) + len(out_specs)
        aliases = dict(aliases or {})
        aliases.update({spot + k: len(out_specs) + k for k in range(len(carry))})
        known = self.last is None or any(self.last is x for x in list(args) + list(carry))
        unread = list(carry) + list(after) + ([] if known else [self.last])
        args += unread
        in_specs += [anywhere] * len(unread)
        out_specs += [anywhere] * len(carry)
        out_shape += [shape_of(c.shape, c.dtype) for c in carry]

        def body(*refs):
            outs_at = spot + len(unread)
            outs_end = outs_at + spot_out - spot
            kernel(*refs[:spot], *refs[outs_at:outs_end], *refs[outs_end + len(carry) :])

        out = pl.pallas_call(
            body,
            grid_spec=pltpu.PrefetchScalarGridSpec(
                num_scalar_prefetch=ahead,
                grid=grid,
                in_specs=in_specs,
                out_specs=list(out_specs),
                scratch_shapes=list(scratch),
            ),
            out_shape=list(out_shape),
            input_output_aliases=aliases,
            compiler_params=pltpu.CompilerParams(
                vmem_limit_bytes=VMEM_LIMIT, dimension_semantics=("arbitrary",)
            ),
            cost_estimate=price,
            name=name,
        )(*args)
        out = list(out)
        self.last = out[0]
        return out


def add(line, a, b):
    count = a.shape[0] if len(a.shape) == 3 else 1
    part = shape_of(a.shape[-2:], BF16)
    out = line(
        add_kernel,
        [a, b],
        [whole(a), whole(b)],
        [whole(part)] * count,
        [part] * count,
        (1,),
        price=cost(a.size, 6 * a.size),
        name="add",
    )
    return out if len(a.shape) == 3 else out[0]


def local(
    tokens,
    ln1_gain,
    ln1_bias,
    w_qkv,
    w_attn_out,
    ln2_gain,
    ln2_bias,
    w_router,
    w_in,
    w_out,
    routes,
    priority,
    cotangent,
    n_exp,
    reps,
):
    images, seq, width = tokens.shape
    tok_count = images * seq
    layers, local_experts, _, hidden = w_in.shape
    experts = n_exp * local_experts
    zs, cores = 4, 2
    xs = reps // (zs * cores)
    n = n_exp * cores
    per = local_experts // cores
    cap = 2 * tok_count // experts
    cp = round_up(cap + 2, 16)
    sp = round_up(seq, 16)
    tiles = zs
    tile = hidden // tiles
    rows_in = width // reps
    rows_out = hidden // reps
    bits = reps.bit_length() - 1
    x_bits = list(range(1, bits - 2))
    z_bits = [bits - 2, bits - 1]
    me_rep = lax.axis_index("rep")
    me_exp = lax.axis_index("exp")
    core = me_rep % cores
    ids = jnp.stack([me_exp, core]).astype(jnp.int32)
    router_wide = jnp.pad(w_router, ((0, 0), (0, 0), (0, LANES - experts)))
    dims = dict(n=n, per=per, cp=cp)

    lanes = round_up(tok_count, LANES)
    line = Line()
    row, col = line(
        partial(route_kernel, cap=cap, images=images, seq=seq, **dims),
        [ids, routes, priority],
        [smem()] + [spec((1, tok_count, 2), lambda l: (l, 0, 0))] * 2,
        [
            spec((1, 8, images * WIDE), lambda l: (l, 0, 0)),
            spec((1, images, sp, LANES), lambda l: (l, 0, 0, 0)),
        ],
        [
            shape_of((layers, 8, images * WIDE), jnp.int32),
            shape_of((layers, images, sp, LANES), jnp.int32),
        ],
        (layers,),
        [pltpu.VMEM((lanes, LANES), jnp.int32), pltpu.VMEM((LANES, WIDE), jnp.int32)],
        cost(4e7, 1e6),
        "route",
    )

    slot_shape = shape_of((cp, width), BF16)
    slot_shapes = [slot_shape] * (n * per)
    slot_specs = [whole(slot_shape)] * (n * per)
    joint_shapes = [shape_of((per * cp, width), BF16)] * n
    joint_specs = [whole(joint_shapes[0])] * n

    def nested(flat):
        return [list(flat[d * per : (d + 1) * per]) for d in range(n)]

    def flat_of(lists):
        return [part for group in lists for part in group]

    axes = ("rep", "exp")

    def shifted(d, back):
        pairs = []
        for r in range(reps):
            for y in range(n_exp):
                there = (r ^ (d % 2)) * n_exp + (y + d // 2) % n_exp
                here = r * n_exp + y
                pairs.append((there, here) if back else (here, there))
        return pairs

    def move(lists, back):
        result = [lists[0]]
        for d in range(1, n):
            result.append([lax.ppermute(part, axes, shifted(d, back)) for part in lists[d]])
        return result

    def go_back(part, d):
        return part if d == 0 else lax.ppermute(part, axes, shifted(d, True))

    def send(lists):
        return move(lists, False)

    def send_back(lists):
        return move(lists, True)

    def col_spec(layer):
        return spec((1, 1, sp, LANES), lambda i: (layer, i, 0, 0))

    row_spec_of = lambda layer: spec((1, 8, images * WIDE), lambda *_: (layer, 0, 0))

    top = layers - 1

    def spread_cotangent():
        return [
            [part]
            for part in line(
                partial(cotangent_kernel, images=images, seq=seq, **dims),
                [ids, cotangent, row],
                [smem(), whole(cotangent), row_spec_of(top)],
                joint_specs,
                joint_shapes,
                (1,),
                [pltpu.VMEM((images * WIDE, width), BF16)],
                cost(2 * n * per * cp * images * WIDE * width, 4e6),
                "spread_cotangent",
            )
        ]

    def run_forward(layer, previous):
        first = layer == 0
        args = [ids]
        specs = [smem()]
        if first:
            args += [tokens]
            specs += [per_image(tokens.shape)]
        else:
            middle, gate, back = previous
            args += [middle, gate, col] + flat_of(back)
            specs += [per_image(middle.shape), per_image(gate.shape), col_spec(layer - 1)] + slot_specs
        args += [ln1_gain, ln1_bias, w_qkv, w_attn_out, ln2_gain, ln2_bias, router_wide, col, row]
        specs += [
            whole(ln1_gain),
            whole(ln1_bias),
            of_layer(w_qkv, layer),
            of_layer(w_attn_out, layer),
            whole(ln2_gain),
            whole(ln2_bias),
            of_layer(router_wide, layer),
            col_spec(layer),
            row_spec_of(layer),
        ]
        shapes = [] if first else [shape_of((images, sp, width), F32)]
        shapes += [
            shape_of((images, sp, 3 * width), BF16),
            shape_of((images, HEADS, sp, sp), BF16),
            shape_of((images, sp, width), BF16),
            shape_of((images, sp, width), F32),
            shape_of((images, sp, width), BF16),
            shape_of((images, sp, LANES), F32),
            shape_of((images, sp, LANES), F32),
        ]
        out_specs = [per_image(s.shape) for s in shapes] + slot_specs
        scratch = [pltpu.VMEM((images * WIDE, width + 2 * LANES), BF16)]
        if first:
            scratch.append(pltpu.VMEM((sp, width), F32))
        out = line(
            partial(
                forward_kernel,
                first=first,
                layer=layer,
                images=images,
                seq=seq,
                experts=experts,
                **dims,
            ),
            args,
            specs,
            out_specs,
            shapes + slot_shapes,
            (images,),
            scratch,
            cost(6e9, 2e7, 1e6),
            "forward",
        )
        state = tokens if first else out.pop(0)
        return state, out[:7], nested(out[7:])

    any_spec = pl.BlockSpec(memory_space=pl.ANY)

    def rows_of(lists, j, args, specs):
        for d in range(n):
            array = lists[d][j] if len(lists[d]) > 1 else lists[d][0]
            at = 0 if len(lists[d]) > 1 else j
            args.append(array)
            specs.append(spec((cp, width), lambda *_, at=at: (at, 0)))

    act_shape = shape_of((n * cp, hidden), BF16)
    act_spec = spec((n * cp, tile), lambda h, *_: (0, h))
    cat_shape = shape_of((n * cp, width), BF16)

    def run_expert(layer, j, x, g, made, produce, backward, earlier=()):
        args, specs = [ids], []
        rows_of(x, j, args, specs)
        if backward:
            rows_of(g, j, args, specs)
            if not produce:
                rows_of(made, j, args, specs)
        for parts in earlier:
            args += parts
            specs += [whole(slot_shape)] * n
        args += [w_in, w_out]
        specs += [
            spec((1, 1, width, tile), lambda h, who: (layer, who[1] * per + j, 0, h)),
            spec((1, 1, tile, width), lambda h, who: (layer, who[1] * per + j, h, 0)),
        ]
        shapes = []
        out_specs = []
        scratch = [pltpu.VMEM((n * cp, width), BF16)]
        if not backward:
            scratch.append(pltpu.VMEM((n * cp, tile), BF16))
        if produce:
            made_shape = shape_of(((1 + len(earlier)) * cp, width), BF16)
            shapes += [made_shape] * n
            out_specs += [whole(made_shape)] * n
            scratch += [pltpu.VMEM((n * cp, width), F32)]
        if backward:
            shapes += [slot_shape] * n + [act_shape] * 2 + [cat_shape]
            out_specs += [whole(slot_shape)] * n + [act_spec] * 2 + [whole(cat_shape)]
            scratch += [pltpu.VMEM((n * cp, width), BF16), pltpu.VMEM((n * cp, width), F32)]
        out = line(
            partial(
                expert_kernel,
                n=n,
                cp=cp,
                tiles=tiles,
                produce=produce,
                backward=backward,
                joined=len(earlier),
            ),
            args,
            specs,
            out_specs,
            shapes,
            (tiles,),
            scratch,
            cost(1, 1),
            "expert",
            1,
        )
        if backward:
            return out[:-3], out[-3:]
        return out, None

    def run_weights(j, x, saved, before=None, after=()):
        args, specs = [ids], []
        rows_of(x, j, args, specs)
        args += saved
        specs += [act_spec] * 2 + [whole(cat_shape)]
        aliases = {}
        if before is not None:
            aliases = {len(args): 0}
            args.append(before)
            specs.append(any_spec)
        return line(
            partial(
                weight_kernel,
                n=n,
                cp=cp,
                tiles=tiles,
                wire=(reps, rows_in, rows_out, j),
                follows=before is not None,
            ),
            args,
            specs,
            [any_spec],
            [shape_of((reps, 2 * per * rows_out, width), BF16)],
            (tiles,),
            [
                pltpu.VMEM((n * cp, width), BF16),
                pltpu.VMEM((reps, rows_out, width), BF16),
                pltpu.VMEM((reps, tiles * rows_in, tile), BF16),
                pltpu.SemaphoreType.DMA((2,)),
            ],
            cost(1, 1),
            "weights",
            1,
            after=after,
            aliases=aliases,
        )[0]

    def dense_steps(mine, other, result):
        parts = add(line, mine, swap(other, "rep", 1, reps))
        yield
        total = parts[0]
        for side in range(1, n_exp):
            total = add(line, total, swap(parts[side], "exp", side, n_exp))
            yield
        result.append(total)
        while True:
            yield

    def dense_over_chips(totals):
        chips = reps // cores
        parts = jnp.stack([t.reshape(chips, t.shape[0] // chips, t.shape[1]) for t in totals], axis=1)
        parts = lax.all_to_all(
            parts, "rep", split_axis=0, concat_axis=0, axis_index_groups=groups, tiled=True
        )
        share = jnp.sum(parts.astype(F32), axis=0, keepdims=True).astype(BF16)
        parts = lax.all_to_all(
            jnp.broadcast_to(share, parts.shape),
            "rep",
            split_axis=0,
            concat_axis=0,
            axis_index_groups=groups,
            tiled=True,
        )
        full = parts.transpose(1, 0, 2, 3).reshape(layers, totals[0].shape[0], totals[0].shape[1])
        return full, swap(full, "rep", 1, reps)

    def step(process):
        next(process, None)

    def run_out(previous):
        middle, gate, back = previous
        back = flat_of(back)
        return line(
            partial(out_kernel, seq=seq, **dims),
            [middle, gate, col] + back,
            [per_image(middle.shape), per_image(gate.shape), col_spec(top)] + [whole(p) for p in back],
            [per_image(tokens.shape)],
            [shape_of(tokens.shape, F32)],
            (images,),
            (),
            cost(2 * images * sp * n * per * cp * width, 6e6),
            "block_out",
        )[0]

    def run_backward(layer, grad, state, cached, d_back, carry):
        first = layer == 0
        last = layer == top
        joined, probs, attended, middle, moe_in, router, gate = cached
        args = [ids, grad, state, joined, probs, attended, middle, moe_in, router, col]
        specs = [smem()] + [per_image(a.shape) for a in args[1:-1]] + [col_spec(layer)]
        args += flat_of(d_back)
        specs += slot_specs
        args += [ln1_gain, ln1_bias, w_qkv, w_attn_out, ln2_gain, router_wide]
        specs += [
            whole(ln1_gain),
            whole(ln1_bias),
            of_layer(w_qkv, layer),
            of_layer(w_attn_out, layer),
            whole(ln2_gain),
            of_layer(router_wide, layer),
        ]
        dense_shape = shape_of((n_exp, width // n, 4 * width + LANES), BF16)
        grad_shape = tokens.shape if first else (images, sp, width)
        shapes = [shape_of(grad_shape, F32), dense_shape, dense_shape]
        out_specs = [per_image(grad_shape), whole(dense_shape), whole(dense_shape)]
        scratch = [
            pltpu.VMEM((n, per, cp, LANES), BF16),
            pltpu.VMEM((width, 3 * width), F32),
            pltpu.VMEM((width, width), F32),
            pltpu.VMEM((width, LANES), F32),
            pltpu.VMEM((8, width), F32),
            pltpu.VMEM((LANES, width), F32),
            pltpu.VMEM((sp, 3 * width), BF16),
        ]
        if last:
            scratch.append(pltpu.VMEM((sp, width), F32))
        if first:
            scratch.append(pltpu.VMEM((sp, width), F32))
        else:
            args.append(row)
            specs.append(row_spec_of(layer - 1))
            shapes += slot_shapes
            out_specs += slot_specs
            scratch.append(pltpu.VMEM((images * WIDE, width), BF16))
        out = line(
            partial(
                backward_kernel,
                first=first,
                last=last,
                layer=layer,
                images=images,
                seq=seq,
                experts=experts,
                **dims,
            ),
            args,
            specs,
            out_specs,
            shapes,
            (images,),
            scratch,
            cost(1.2e10, 3e7, 0),
            "backward",
            carry=carry,
        )
        count = len(out) - len(carry)
        return out[0], out[1:3], nested(out[3:count]), out[count:]

    kept = []
    previous = None
    for layer in range(layers):
        if layer == top:
            g_rows = send(spread_cotangent())
        state, cached, rows_sent = run_forward(layer, previous)
        x = send(rows_sent)
        made = [[] for _ in range(n)]
        if layer < top:
            for j in range(per):
                out, _ = run_expert(layer, j, x, None, None, True, False)
                for d in range(n):
                    made[d].append(out[d])
            previous = (cached[3], cached[6], send_back(made))
        kept.append((state, cached, x, made))

    state, cached, x, _ = kept[top]
    outs, saved = [], []
    d_back = [[] for _ in range(n)]
    for j in range(per):
        earlier = [o[:n] for o in outs] if j == per - 1 else ()
        out, kept_rows = run_expert(top, j, x, g_rows, None, True, True, earlier)
        outs.append(out)
        saved.append(kept_rows)
        for d, part in enumerate(out[n : 2 * n]):
            d_back[d].append(go_back(part, d))
    groups = [[r for r in range(reps) if r % cores == c] for c in range(cores)]

    def summed(x, saved):
        wire = None
        for j in range(per):
            wire = run_weights(j, x, saved[j], wire)
        share = lax.psum_scatter(
            wire, "rep", scatter_dimension=0, axis_index_groups=groups, tiled=True
        )
        half = share.shape[0] // 2
        return share[:half], swap(share[half:], "rep", 1, reps)

    shares = [None] * layers
    dense = [[] for _ in range(layers)]
    shares[top] = summed(x, saved)
    grad, parts, g_rows, _ = run_backward(top, cotangent, state, cached, d_back, ())
    g_rows = send(g_rows)
    flow_top = dense_steps(parts[0], parts[1], dense[top])
    back_top = send_back([[part] for part in outs[-1][:n]])
    block_out = run_out((cached[3], cached[6], back_top))

    state, cached, x, made = kept[0]
    d_back = [[] for _ in range(n)]
    saved = []
    for j in range(per):
        out, kept_rows = run_expert(0, j, x, g_rows, made, False, True)
        saved.append(kept_rows)
        for k in range(n):
            d_back[k].append(go_back(out[k], k))
        if j == 0:
            step(flow_top)
    shares[0] = summed(x, saved)
    grad, parts, _, _ = run_backward(0, grad, state, cached, d_back, ())
    flow = dense_steps(parts[0], parts[1], dense[0])
    step(flow)
    while not dense[top]:
        step(flow_top)
    while not dense[0]:
        step(flow)
    halves = list(dense_over_chips([d[0] for d in dense]))
    rows = width // n_exp
    dense_shapes = [
        shape_of((layers, rows, 3 * width), F32),
        shape_of((layers, rows, width), F32),
        shape_of((layers, rows, experts), F32),
    ] + [shape_of((layers, rows), F32)] * 4
    qkv, attn_out, router, gain1, bias1, gain2, bias2 = line(
        partial(dense_kernel, layers=layers, width=width, experts=experts),
        [ids] + halves,
        [smem()] + [whole(p) for p in halves],
        [whole(s) for s in dense_shapes],
        dense_shapes,
        (1,),
        [pltpu.VMEM((WIDE, LANES), F32)],
        cost(1e6, 6e6),
        "finish_dense",
    )
    pieces = [part for pair in shares for part in pair]
    in_shape = shape_of((layers, local_experts, rows_in, hidden), F32)
    out_shape = shape_of((layers, local_experts, rows_out, width), F32)
    grad_in, grad_out = line(
        partial(finish_kernel, layers=layers, pairs=per, tiles=tiles, rows_in=rows_in),
        [ids] + pieces,
        [smem()] + [whole(p) for p in pieces],
        [whole(in_shape), whole(out_shape)],
        [in_shape, out_shape],
        (1,),
        (),
        cost(1e6, 6e6),
        "finish",
    )
    return (
        block_out,
        grad,
        gain1,
        bias1,
        qkv,
        attn_out,
        gain2,
        bias2,
        router,
        grad_in,
        grad_out,
    )


def solution(mesh):
    return jax.shard_map(
        partial(local, n_exp=mesh.shape["exp"], reps=mesh.shape["rep"]),
        mesh=mesh,
        in_specs=(
            P(("rep", "exp"), None, None),
            P(),
            P(),
            P(),
            P(),
            P(),
            P(),
            P(),
            P(None, "exp", None, None),
            P(None, "exp", None, None),
            P(None, ("rep", "exp"), None),
            P(None, ("rep", "exp"), None),
            P(("rep", "exp"), None, None),
        ),
        out_specs=(
            P(("rep", "exp"), None, None),
            P(("rep", "exp"), None, None),
            P(None, "exp"),
            P(None, "exp"),
            P(None, "exp", None),
            P(None, "exp", None),
            P(None, "exp"),
            P(None, "exp"),
            P(None, "exp", None),
            P(None, "exp", "rep", None),
            P(None, "exp", "rep", None),
        ),
        check_vma=False,
    )
```

```python
from functools import partial

import jax
import jax.numpy as jnp
from jax import lax
from jax.experimental import pallas as pl
from jax.experimental.pallas import tpu as pltpu
from jax.sharding import PartitionSpec as P

HEADS = 8
HEAD_DIM = 64
EPSILON = 1e-06
LANES = 128
WIDE = 256
F32 = jnp.float32
BF16 = jnp.bfloat16
VMEM_LIMIT = 40 * 1024 * 1024


def round_up(value, multiple):
    return -(-value // multiple) * multiple


def nn(a, b):
    return lax.dot_general(a, b, (((1,), (0,)), ((), ())), preferred_element_type=F32)


def nt(a, b):
    return lax.dot_general(a, b, (((1,), (1,)), ((), ())), preferred_element_type=F32)


def tn(a, b):
    return lax.dot_general(a, b, (((0,), (0,)), ((), ())), preferred_element_type=F32)


def iota(shape, dim):
    return lax.broadcasted_iota(jnp.int32, shape, dim)


def row_to_col(row, rows):
    shape = (rows, row.shape[1])
    return jnp.sum(jnp.where(iota(shape, 0) == iota(shape, 1), row, 0.0), axis=1, keepdims=True)


def col_to_row(col, lanes):
    shape = (col.shape[0], lanes)
    return jnp.sum(jnp.where(iota(shape, 0) == iota(shape, 1), col, 0.0), axis=0, keepdims=True)


def normalized(values):
    average = jnp.mean(values, axis=-1, keepdims=True)
    centred = values - average
    spread = jnp.mean(centred * centred, axis=-1, keepdims=True)
    factor = lax.rsqrt(spread + EPSILON)
    return centred * factor, factor


def norm_back(grad, gain, xhat, factor):
    scaled = grad * gain
    mean_e = jnp.mean(scaled, axis=-1, keepdims=True)
    mean_x = jnp.mean(scaled * xhat, axis=-1, keepdims=True)
    return factor * (scaled - mean_e - xhat * mean_x)


def gelu_both(x):
    phi = 0.5 + 0.5 * lax.erf(x * 0.7071067811865476)
    raised = jnp.exp2((x * x) * -0.7213475204444817)
    return x * phi, phi + x * raised * 0.3989422804014327


def route_kernel(ids, r_ref, p_ref, row_ref, col_ref, tall, wide, *, n, per, cap, cp, images, seq):
    tokens = images * seq
    bits = (2 * tokens - 1).bit_length()
    my_exp, my_core = ids[0], ids[1]
    key = (r_ref[0] << bits) + p_ref[0]
    tall[...] = jnp.full(tall.shape, -1, jnp.int32)
    tall[0:tokens, 0:2] = key
    flipped = tall[...].T
    lanes = tall.shape[0]
    slots = []
    experts = []
    for k in range(2):
        mine = flipped[k : k + 1, :]
        expert = mine >> bits
        least = expert << bits
        count = jnp.zeros((1, lanes), jnp.int32)
        for other in range(2):
            theirs = key[:, other : other + 1]
            hit = jnp.logical_and(theirs >= least, theirs < mine)
            count = count + jnp.sum(jnp.where(hit, 1, 0), axis=0, keepdims=True)
        group = jnp.zeros((1, lanes), jnp.int32)
        for q in range(1, n):
            group = group + jnp.where(expert >= q * per, 1, 0)
        ahead = (group >> 1) - my_exp
        ahead = jnp.where(ahead < 0, ahead + n // 2, ahead)
        ahead = 2 * ahead + jnp.where((group & 1) == my_core, 0, 1)
        slot = (ahead * per + (expert - group * per)) * cp + count
        kept = count < cap
        slots.append(jnp.where(kept, slot, -1))
        experts.append(jnp.where(kept, expert, -1))
    table = jnp.concatenate(slots + experts + [jnp.full((4, lanes), -1, jnp.int32)], axis=0)
    sp = col_ref.shape[2]
    for i in range(images):
        moved = table if i == 0 else pltpu.roll(table, lanes - seq * i, axis=1)
        piece = moved[:, :WIDE]
        piece = jnp.where(iota(piece.shape, 1) < seq, piece, -1)
        row_ref[0, :, i * WIDE : (i + 1) * WIDE] = piece
        wide[0:8, :] = piece
        col_ref[0, i] = wide[...].T[0:sp, :]


def first_expert(ids, d, n, per):
    side = lax.rem(ids[0] + d // 2, n // 2)
    core = ids[1] if d % 2 == 0 else 1 - ids[1]
    return (2 * side + core) * per


def spread_rows(ids, row_ref, rhs, outs, n, per, cp, width, experts):
    slots0 = row_ref[0, 0:1, :]
    slots1 = row_ref[0, 1:2, :]
    shape = (per * cp, row_ref.shape[2])
    for d in list(range(1, n)) + [0]:
        place = iota(shape, 0) + d * per * cp
        pick = jnp.where(jnp.logical_or(place == slots0, place == slots1), 1.0, 0.0).astype(BF16)
        rows = nn(pick, rhs[...])
        base = first_expert(ids, d, n, per)
        for j in range(per):
            part = rows[j * cp : (j + 1) * cp, :]
            data = part[:, :width]
            if experts:
                both = part[:, width : width + LANES] + part[:, width + LANES :]
                gate = jnp.sum(
                    jnp.where(iota(both.shape, 1) == base + j, both, 0.0), axis=1, keepdims=True
                )
                line = col_to_row(gate, width)
                high = line.astype(BF16).astype(F32)
                where = iota(data.shape, 0)
                data = jnp.where(where == cp - 1, high, data)
                data = jnp.where(where == cp - 2, line - high, data)
            if len(outs[d]) == per:
                outs[d][j][...] = data.astype(BF16)
            else:
                outs[d][0][j * cp : (j + 1) * cp, :] = data.astype(BF16)


def gathered(c0, c1, v0, v1, back, n, per, cp):
    shape = (c0.shape[0], cp)
    place = iota(shape, 1)
    total = None
    for d in range(n):
        for j in range(per):
            base = (d * per + j) * cp
            pick = jnp.where(c0 - base == place, v0, 0.0) + jnp.where(c1 - base == place, v1, 0.0)
            term = nn(pick.astype(BF16), back[d][j][...])
            total = term if total is None else total + term
    return total


def take(it, n, per):
    return [[next(it) for _ in range(per)] for _ in range(n)]


def head_masks():
    lane = iota((1, LANES), 1)
    low = jnp.where(lane < HEAD_DIM, 1.0, 0.0).astype(BF16)
    high = jnp.where(lane < HEAD_DIM, 0.0, 1.0).astype(BF16)
    return low, high


def forward_kernel(*refs, first, layer, n, per, cp, images, seq, experts):
    it = iter(refs)
    ids = next(it)
    if first:
        x_ref = next(it)
    else:
        mid_in, gate_in, col_in = next(it), next(it), next(it)
        back = take(it, n, per)
    g1, b1, wqkv, wo, g2, b2, wr, col, row = (next(it) for _ in range(9))
    if not first:
        state_out = next(it)
    joined_out, probs_out, attended_out, middle_out, moe_out, rp_out, gate_out = (
        next(it) for _ in range(7)
    )
    disp = take(it, n, per)
    rhs = next(it)
    i = pl.program_id(0)
    sp = middle_out.shape[1]
    width = middle_out.shape[2]

    @pl.when(i == 0)
    def _():
        rhs[...] = jnp.zeros(rhs.shape, BF16)

    if first:
        xs = next(it)

        @pl.when(i == 0)
        def _():
            xs[...] = jnp.zeros(xs.shape, F32)

        xs[0:seq, :] = x_ref[0]
        state = xs[...]
    else:
        state = mid_in[0] + gathered(
            col_in[0, 0, :, 0:1],
            col_in[0, 0, :, 1:2],
            gate_in[0, :, 0:1],
            gate_in[0, :, 1:2],
            back,
            n,
            per,
            cp,
        )
        state_out[0] = state
    xhat, _ = normalized(state)
    normed = (xhat * g1[layer : layer + 1, :] + b1[layer : layer + 1, :]).astype(BF16)
    joined = nn(normed, wqkv[0]).astype(BF16)
    joined_out[0] = joined
    masks = head_masks()
    valid = iota((1, sp), 1) < seq
    pieces = []
    for pair in range(HEADS // 2):
        at = pair * LANES
        q = joined[:, at : at + LANES]
        k = joined[:, width + at : width + at + LANES]
        v = joined[:, 2 * width + at : 2 * width + at + LANES]
        mixed = None
        for half in range(2):
            scores = jnp.where(valid, nt(q, k * masks[half]), -1e30)
            top = jnp.max(scores, axis=-1, keepdims=True)
            raised = jnp.exp((scores - top) * HEAD_DIM ** (-0.5))
            total = jnp.sum(raised, axis=-1, keepdims=True)
            probs = (raised * (1.0 / total)).astype(BF16)
            probs_out[0, 2 * pair + half] = probs
            term = nn(probs, v * masks[half])
            mixed = term if mixed is None else mixed + term
        pieces.append(mixed.astype(BF16))
    attended = jnp.concatenate(pieces, axis=1)
    attended_out[0] = attended
    middle = state + nn(attended, wo[0])
    middle_out[0] = middle
    xhat, _ = normalized(middle)
    moe_in = (xhat * g2[layer : layer + 1, :] + b2[layer : layer + 1, :]).astype(BF16)
    moe_out[0] = moe_in
    logits = nn(moe_in, wr[0])
    lane = iota(logits.shape, 1)
    logits = jnp.where(lane < experts, logits, -1e30)
    raised = jnp.exp(logits - jnp.max(logits, axis=-1, keepdims=True))
    router = raised * (1.0 / jnp.sum(raised, axis=-1, keepdims=True))
    rp_out[0] = router
    gates = []
    for k in range(2):
        chosen = col[0, 0, :, 2 + k : 3 + k]
        gates.append(jnp.sum(jnp.where(lane == chosen, router, 0.0), axis=1, keepdims=True))
    gate_out[0] = jnp.where(lane == 0, gates[0], jnp.where(lane == 1, gates[1], 0.0))
    high = router.astype(BF16)
    low = (router - high.astype(F32)).astype(BF16)
    at = pl.multiple_of(i * WIDE, WIDE)
    rhs[pl.ds(at, sp), 0:width] = moe_in
    rhs[pl.ds(at, sp), width : width + LANES] = high
    rhs[pl.ds(at, sp), width + LANES : width + 2 * LANES] = low

    @pl.when(i == images - 1)
    def _():
        spread_rows(ids, row, rhs, disp, n, per, cp, width, experts)


def cotangent_kernel(*refs, n, per, cp, images, seq):
    it = iter(refs)
    ids, g_ref, row = next(it), next(it), next(it)
    outs = take(it, n, 1)
    rhs = next(it)
    rhs[...] = jnp.zeros(rhs.shape, BF16)
    for i in range(images):
        rhs[i * WIDE : i * WIDE + seq, :] = g_ref[i].astype(BF16)
    spread_rows(ids, row, rhs, outs, n, per, cp, rhs.shape[1], 0)


def out_kernel(*refs, n, per, cp, seq):
    it = iter(refs)
    mid, gate, col = next(it), next(it), next(it)
    joint = take(it, n, 1)
    back = [[part[0].at[pl.ds(j * cp, cp)] for j in range(per)] for part in joint]
    out = next(it)
    state = mid[0] + gathered(
        col[0, 0, :, 0:1], col[0, 0, :, 1:2], gate[0, :, 0:1], gate[0, :, 1:2], back, n, per, cp
    )
    out[0] = state[0:seq, :]


def slot_gates(rows, cp):
    tail = rows[cp - 16 : cp, 0:WIDE].astype(F32)
    line = jnp.sum(jnp.where(iota(tail.shape, 0) >= 14, tail, 0.0), axis=0, keepdims=True)
    return row_to_col(line, cp)


def expert_kernel(*refs, n, cp, tiles, produce, backward, joined):
    it = iter(refs)
    next(it)
    xs = [next(it) for _ in range(n)]
    if backward:
        gs = [next(it) for _ in range(n)]
        if not produce:
            made = [next(it) for _ in range(n)]
    earlier = [[next(it) for _ in range(n)] for _ in range(joined)]
    w_in, w_out = next(it), next(it)
    if produce:
        prod = [next(it) for _ in range(n)]
    if backward:
        dx = [next(it) for _ in range(n)]
        act_s, dpre_s, dprod_out = next(it), next(it), next(it)
    xcat = next(it)
    if not backward:
        act_s = next(it)
    if produce:
        acc_p = next(it)
    if backward:
        dprod, acc_d = next(it), next(it)
    h = pl.program_id(0)
    width = xcat.shape[1]

    @pl.when(h == 0)
    def _():
        for d in range(n):
            xcat[d * cp : (d + 1) * cp, :] = xs[d][...]
            if backward:
                gate = slot_gates(xs[d], cp)
                part = (gate * gs[d][...].astype(F32)).astype(BF16)
                dprod[d * cp : (d + 1) * cp, :] = part
                dprod_out[d * cp : (d + 1) * cp, :] = part
        if produce:
            acc_p[...] = jnp.zeros(acc_p.shape, F32)
        if backward:
            acc_d[...] = jnp.zeros(acc_d.shape, F32)

    step = 16
    pre = nn(xcat[...], w_in[0, 0])
    if backward:
        d_act = nt(dprod[...], w_out[0, 0])
    for r in range(0, n * cp, step):
        rows = slice(r, r + step)
        value, slope = gelu_both(pre[rows, :])
        act_s[rows, :] = value.astype(BF16)
        if backward:
            dpre_s[rows, :] = (d_act[rows, :] * slope).astype(BF16)
    if produce:
        acc_p[...] += nn(act_s[...], w_out[0, 0])
    if backward:
        acc_d[...] += nt(dpre_s[...], w_in[0, 0])

    @pl.when(h == tiles - 1)
    def _():
        for d in range(n):
            rows = pl.ds(d * cp, cp)
            if produce:
                result = acc_p[rows, :].astype(BF16)
                prod[d][joined * cp :, :] = result
                for k in range(joined):
                    prod[d][k * cp : (k + 1) * cp, :] = earlier[k][d][...]
            if backward:
                if not produce:
                    result = made[d][...]
                d_gate = jnp.sum(
                    result.astype(F32) * gs[d][...].astype(F32), axis=1, keepdims=True
                )
                line = col_to_row(d_gate, width)
                data = acc_d[rows, :]
                dx[d][...] = jnp.where(iota(data.shape, 0) == cp - 1, line, data).astype(BF16)


def weight_kernel(*refs, n, cp, tiles, wire, follows):
    it = iter(refs)
    ids = next(it)
    xs = [next(it) for _ in range(n)]
    act, dpre, dprod = next(it), next(it), next(it)
    if follows:
        next(it)
    reps, rows_in, rows_out, spot_at = wire
    target = next(it)
    xcat, wires, sems = next(it), [next(it), next(it)], next(it)
    h = pl.program_id(0)

    @pl.when(h == 0)
    def _():
        for d in range(n):
            xcat[d * cp : (d + 1) * cp, :] = xs[d][...]

    grad_out = tn(act[...], dprod[...]).astype(BF16)
    for q in range(reps // tiles):
        spot = (h * (reps // tiles) + q) ^ ids[1]
        wires[0][spot] = grad_out[q * rows_out : (q + 1) * rows_out, :]
    grad_in = tn(xcat[...], dpre[...]).astype(BF16)
    line = pl.multiple_of(h * rows_in, rows_in)
    for q in range(reps):
        wires[1][q ^ ids[1], pl.ds(line, rows_in), :] = grad_in[q * rows_in : (q + 1) * rows_in, :]

    @pl.when(h == tiles - 1)
    def _():
        rows = wires[0].shape[1]
        copies = [
            pltpu.make_async_copy(
                wires[k], target.at[:, pl.ds((2 * spot_at + k) * rows, rows)], sems.at[k]
            )
            for k in range(2)
        ]
        for copy in copies:
            copy.start()
        for copy in copies:
            copy.wait()


def finish_kernel(*refs, layers, pairs, tiles, rows_in):
    it = iter(refs)
    ids = next(it)
    parts = [(next(it), next(it)) for _ in range(layers)]
    grad_in, grad_out = next(it), next(it)
    rows, tile = grad_out.shape[2:]
    for layer in range(layers):
        for j in range(pairs):
            for side in range(2):
                core = ids[1] if side == 0 else 1 - ids[1]
                expert = core * pairs + j
                part = parts[layer][side]
                at = 2 * j * rows
                grad_out[layer, expert] = part[0, at : at + rows, :].astype(F32)
                for h in range(tiles):
                    line = at + rows + h * rows_in
                    grad_in[layer, expert, :, h * tile : (h + 1) * tile] = part[
                        0, line : line + rows_in, :
                    ].astype(F32)


def add_kernel(*refs):
    a, b, outs = refs[0], refs[1], refs[2:]
    for k, out in enumerate(outs):
        one, two = (a, b) if len(a.shape) == 2 else (a.at[k], b.at[k])
        out[...] = (one[...].astype(F32) + two[...].astype(F32)).astype(BF16)


def dense_kernel(*refs, layers, width, experts):
    it = iter(refs)
    ids = next(it)
    parts = [next(it), next(it)]
    qkv, out, router = next(it), next(it), next(it)
    norms = [next(it) for _ in range(4)]
    tall = next(it)
    half = parts[0].shape[1]
    for layer in range(layers):
        for side in range(2):
            core = ids[1] if side == 0 else 1 - ids[1]
            rows = pl.ds(pl.multiple_of(core * half, half), half)
            part = parts[side].at[layer]
            qkv[layer, rows, :] = part[:, 0 : 3 * width].astype(F32)
            out[layer, rows, :] = part[:, 3 * width : 4 * width].astype(F32)
            small = part[:, 4 * width :].astype(F32)
            router[layer, rows, :] = small[:, 0:experts]
            tall[rows, :] = small
        flipped = tall[...].T
        for k in range(4):
            norms[k][layer : layer + 1, :] = flipped[experts + k : experts + k + 1, 0 : 2 * half]


def backward_kernel(*refs, first, last, layer, n, per, cp, images, seq, experts):
    it = iter(refs)
    ids, g_ref, s_ref = next(it), next(it), next(it)
    joined_in, probs_in, attended_in, middle_in, moe_in, rp_in, col = (next(it) for _ in range(7))
    back = take(it, n, per)
    g1, b1, wqkv, wo, g2, wr = (next(it) for _ in range(6))
    if not first:
        row = next(it)
    g_out = next(it)
    dense = [next(it), next(it)]
    if not first:
        outs = take(it, n, per)
    d_cols, a_qkv, a_out, a_router, stats, flip, d_join = (next(it) for _ in range(7))
    if last:
        g_pad = next(it)
    if first:
        s_pad = next(it)
    else:
        rhs = next(it)
    i = pl.program_id(0)
    sp = middle_in.shape[1]
    width = middle_in.shape[2]

    @pl.when(i == 0)
    def _():
        a_qkv[...] = jnp.zeros(a_qkv.shape, F32)
        a_out[...] = jnp.zeros(a_out.shape, F32)
        a_router[...] = jnp.zeros(a_router.shape, F32)
        stats[...] = jnp.zeros(stats.shape, F32)
        flip[...] = jnp.zeros(flip.shape, F32)
        if last:
            g_pad[...] = jnp.zeros(g_pad.shape, F32)
        if first:
            s_pad[...] = jnp.zeros(s_pad.shape, F32)
        else:
            rhs[...] = jnp.zeros(rhs.shape, BF16)
        for d in range(n):
            base = first_expert(ids, d, n, per)
            for j in range(per):
                tail = back[d][j][cp - 16 : cp, 0:WIDE].astype(F32)
                line = jnp.sum(jnp.where(iota(tail.shape, 0) == 15, tail, 0.0), axis=0, keepdims=True)
                column = row_to_col(line, cp)
                d_cols[d, j] = jnp.where(iota((cp, LANES), 1) == base + j, column, 0.0).astype(BF16)

    if last:
        g_pad[0:seq, :] = g_ref[0]
        g = g_pad[...]
    else:
        g = g_ref[0]
    if first:
        s_pad[0:seq, :] = s_ref[0]
        state = s_pad[...]
    else:
        state = s_ref[0]

    c0 = col[0, 0, :, 0:1]
    c1 = col[0, 0, :, 1:2]
    place = iota((sp, cp), 1)
    d_moe = None
    d_rp = None
    for d in range(n):
        for j in range(per):
            base = (d * per + j) * cp
            pick = jnp.where(jnp.logical_or(c0 - base == place, c1 - base == place), 1.0, 0.0)
            pick = pick.astype(BF16)
            term = nn(pick, back[d][j][...])
            small = nn(pick, d_cols[d, j])
            d_moe = term if d_moe is None else d_moe + term
            d_rp = small if d_rp is None else d_rp + small
    router = rp_in[0]
    d_logits = router * (d_rp - jnp.sum(d_rp * router, axis=-1, keepdims=True))
    d_logits = d_logits.astype(BF16)
    a_router[...] += tn(moe_in[0], d_logits)
    d_moe = d_moe + nt(d_logits, wr[0])
    xhat, factor = normalized(middle_in[0])
    stats[2:3, :] += jnp.sum(d_moe * xhat, axis=0, keepdims=True)
    stats[3:4, :] += jnp.sum(d_moe, axis=0, keepdims=True)
    d_middle = g + norm_back(d_moe, g2[layer : layer + 1, :], xhat, factor)
    d_branch = d_middle.astype(BF16)
    a_out[...] += tn(attended_in[0], d_branch)
    d_att = nt(d_branch, wo[0]).astype(BF16)
    masks = head_masks()
    scale = HEAD_DIM ** (-0.5)
    for pair in range(HEADS // 2):
        at = pair * LANES
        q = joined_in[0, :, at : at + LANES]
        k = joined_in[0, :, width + at : width + at + LANES]
        v = joined_in[0, :, 2 * width + at : 2 * width + at + LANES]
        do = d_att[:, at : at + LANES]
        dq = dk = dv = None
        for half in range(2):
            low = probs_in[0, 2 * pair + half]
            probs = low.astype(F32)
            dp = nt(do, v * masks[half])
            ds = (probs * (dp - jnp.sum(dp * probs, axis=-1, keepdims=True))).astype(BF16)
            terms = (
                nn(ds, k * masks[half]),
                tn(ds, q * masks[half]),
                tn(low, do * masks[half]),
            )
            if half == 0:
                dq, dk, dv = terms
            else:
                dq, dk, dv = dq + terms[0], dk + terms[1], dv + terms[2]
        d_join[:, at : at + LANES] = (dq * scale).astype(BF16)
        d_join[:, width + at : width + at + LANES] = (dk * scale).astype(BF16)
        d_join[:, 2 * width + at : 2 * width + at + LANES] = dv.astype(BF16)
    xhat, factor = normalized(state)
    normed = (xhat * g1[layer : layer + 1, :] + b1[layer : layer + 1, :]).astype(BF16)
    a_qkv[...] += tn(normed, d_join[...])
    d_normed = nt(d_join[...], wqkv[0])
    stats[0:1, :] += jnp.sum(d_normed * xhat, axis=0, keepdims=True)
    stats[1:2, :] += jnp.sum(d_normed, axis=0, keepdims=True)
    result = d_middle + norm_back(d_normed, g1[layer : layer + 1, :], xhat, factor)
    if first:
        g_out[0] = result[0:seq, :]
    else:
        g_out[0] = result
        rhs[pl.ds(pl.multiple_of(i * WIDE, WIDE), sp), :] = result.astype(BF16)

    @pl.when(i == images - 1)
    def _():
        if not first:
            spread_rows(ids, row, rhs, outs, n, per, cp, width, 0)
        flip[experts : experts + 8, :] = stats[...]
        a_router[...] += flip[...].T
        half = dense[0].shape[1]
        for core in range(2):

            @pl.when(ids[1] == core)
            def _():
                for side in range(n // 2):
                    spot = ids[0] ^ side
                    for target, c in ((dense[0], core), (dense[1], 1 - core)):
                        rows = slice((2 * side + c) * half, (2 * side + c + 1) * half)
                        target[spot, :, 0 : 3 * width] = a_qkv[rows, :].astype(BF16)
                        target[spot, :, 3 * width : 4 * width] = a_out[rows, :].astype(BF16)
                        target[spot, :, 4 * width :] = a_router[rows, :].astype(BF16)


def spec(shape, index):
    return pl.BlockSpec(shape, index)


def whole(array):
    zeros = (0,) * len(array.shape)
    return pl.BlockSpec(tuple(array.shape), lambda *_: zeros)


def smem():
    return pl.BlockSpec(memory_space=pltpu.SMEM)


def shape_of(shape, dtype):
    return jax.ShapeDtypeStruct(tuple(shape), dtype)


def cost(flops, moved, special=0):
    return pl.CostEstimate(flops=int(flops), bytes_accessed=int(moved), transcendentals=int(special))


def per_image(shape):
    rest = (0,) * (len(shape) - 1)
    return pl.BlockSpec((1,) + tuple(shape[1:]), lambda i: (i,) + rest)


def of_layer(array, layer):
    rest = (0,) * (len(array.shape) - 1)
    return pl.BlockSpec((1,) + tuple(array.shape[1:]), lambda *_: (layer,) + rest)


def swap(values, axis, distance, total):
    return lax.ppermute(values, axis, [(r, r ^ distance) for r in range(total)])


class Line:
    def __init__(self):
        self.last = None

    def __call__(
        self, kernel, args, in_specs, out_specs, out_shape, grid, scratch=(), price=None, name=None, ahead=0, carry=(), after=(), aliases=None
    ):
        anywhere = pl.BlockSpec(memory_space=pl.ANY)
        args, in_specs = list(args), list(in_specs)
        out_specs, out_shape = list(out_specs), list(out_shape)
        spot, spot_out = len(args), len(args) + len(out_specs)
        aliases = dict(aliases or {})
        aliases.update({spot + k: len(out_specs) + k for k in range(len(carry))})
        known = self.last is None or any(self.last is x for x in list(args) + list(carry))
        unread = list(carry) + list(after) + ([] if known else [self.last])
        args += unread
        in_specs += [anywhere] * len(unread)
        out_specs += [anywhere] * len(carry)
        out_shape += [shape_of(c.shape, c.dtype) for c in carry]

        def body(*refs):
            outs_at = spot + len(unread)
            outs_end = outs_at + spot_out - spot
            kernel(*refs[:spot], *refs[outs_at:outs_end], *refs[outs_end + len(carry) :])

        out = pl.pallas_call(
            body,
            grid_spec=pltpu.PrefetchScalarGridSpec(
                num_scalar_prefetch=ahead,
                grid=grid,
                in_specs=in_specs,
                out_specs=list(out_specs),
                scratch_shapes=list(scratch),
            ),
            out_shape=list(out_shape),
            input_output_aliases=aliases,
            compiler_params=pltpu.CompilerParams(
                vmem_limit_bytes=VMEM_LIMIT, dimension_semantics=("arbitrary",)
            ),
            cost_estimate=price,
            name=name,
        )(*args)
        out = list(out)
        self.last = out[0]
        return out


def add(line, a, b):
    count = a.shape[0] if len(a.shape) == 3 else 1
    part = shape_of(a.shape[-2:], BF16)
    out = line(
        add_kernel,
        [a, b],
        [whole(a), whole(b)],
        [whole(part)] * count,
        [part] * count,
        (1,),
        price=cost(a.size, 6 * a.size),
        name="add",
    )
    return out if len(a.shape) == 3 else out[0]


def local(
    tokens,
    ln1_gain,
    ln1_bias,
    w_qkv,
    w_attn_out,
    ln2_gain,
    ln2_bias,
    w_router,
    w_in,
    w_out,
    routes,
    priority,
    cotangent,
    n_exp,
    reps,
):
    images, seq, width = tokens.shape
    tok_count = images * seq
    layers, local_experts, _, hidden = w_in.shape
    experts = n_exp * local_experts
    zs, cores = 4, 2
    xs = reps // (zs * cores)
    n = n_exp * cores
    per = local_experts // cores
    cap = 2 * tok_count // experts
    cp = round_up(cap + 2, 16)
    sp = round_up(seq, 16)
    tiles = zs
    tile = hidden // tiles
    rows_in = width // reps
    rows_out = hidden // reps
    bits = reps.bit_length() - 1
    x_bits = list(range(1, bits - 2))
    z_bits = [bits - 2, bits - 1]
    me_rep = lax.axis_index("rep")
    me_exp = lax.axis_index("exp")
    core = me_rep % cores
    ids = jnp.stack([me_exp, core]).astype(jnp.int32)
    router_wide = jnp.pad(w_router, ((0, 0), (0, 0), (0, LANES - experts)))
    dims = dict(n=n, per=per, cp=cp)

    lanes = round_up(tok_count, LANES)
    line = Line()
    row, col = line(
        partial(route_kernel, cap=cap, images=images, seq=seq, **dims),
        [ids, routes, priority],
        [smem()] + [spec((1, tok_count, 2), lambda l: (l, 0, 0))] * 2,
        [
            spec((1, 8, images * WIDE), lambda l: (l, 0, 0)),
            spec((1, images, sp, LANES), lambda l: (l, 0, 0, 0)),
        ],
        [
            shape_of((layers, 8, images * WIDE), jnp.int32),
            shape_of((layers, images, sp, LANES), jnp.int32),
        ],
        (layers,),
        [pltpu.VMEM((lanes, LANES), jnp.int32), pltpu.VMEM((LANES, WIDE), jnp.int32)],
        cost(4e7, 1e6),
        "route",
    )

    slot_shape = shape_of((cp, width), BF16)
    slot_shapes = [slot_shape] * (n * per)
    slot_specs = [whole(slot_shape)] * (n * per)
    joint_shapes = [shape_of((per * cp, width), BF16)] * n
    joint_specs = [whole(joint_shapes[0])] * n

    def nested(flat):
        return [list(flat[d * per : (d + 1) * per]) for d in range(n)]

    def flat_of(lists):
        return [part for group in lists for part in group]

    axes = ("rep", "exp")

    def shifted(d, back):
        pairs = []
        for r in range(reps):
            for y in range(n_exp):
                there = (r ^ (d % 2)) * n_exp + (y + d // 2) % n_exp
                here = r * n_exp + y
                pairs.append((there, here) if back else (here, there))
        return pairs

    def move(lists, back):
        result = [lists[0]]
        for d in range(1, n):
            result.append([lax.ppermute(part, axes, shifted(d, back)) for part in lists[d]])
        return result

    def go_back(part, d):
        return part if d == 0 else lax.ppermute(part, axes, shifted(d, True))

    def send(lists):
        return move(lists, False)

    def send_back(lists):
        return move(lists, True)

    def col_spec(layer):
        return spec((1, 1, sp, LANES), lambda i: (layer, i, 0, 0))

    row_spec_of = lambda layer: spec((1, 8, images * WIDE), lambda *_: (layer, 0, 0))

    top = layers - 1

    def spread_cotangent():
        return [
            [part]
            for part in line(
                partial(cotangent_kernel, images=images, seq=seq, **dims),
                [ids, cotangent, row],
                [smem(), whole(cotangent), row_spec_of(top)],
                joint_specs,
                joint_shapes,
                (1,),
                [pltpu.VMEM((images * WIDE, width), BF16)],
                cost(2 * n * per * cp * images * WIDE * width, 4e6),
                "spread_cotangent",
            )
        ]

    def run_forward(layer, previous):
        first = layer == 0
        args = [ids]
        specs = [smem()]
        if first:
            args += [tokens]
            specs += [per_image(tokens.shape)]
        else:
            middle, gate, back = previous
            args += [middle, gate, col] + flat_of(back)
            specs += [per_image(middle.shape), per_image(gate.shape), col_spec(layer - 1)] + slot_specs
        args += [ln1_gain, ln1_bias, w_qkv, w_attn_out, ln2_gain, ln2_bias, router_wide, col, row]
        specs += [
            whole(ln1_gain),
            whole(ln1_bias),
            of_layer(w_qkv, layer),
            of_layer(w_attn_out, layer),
            whole(ln2_gain),
            whole(ln2_bias),
            of_layer(router_wide, layer),
            col_spec(layer),
            row_spec_of(layer),
        ]
        shapes = [] if first else [shape_of((images, sp, width), F32)]
        shapes += [
            shape_of((images, sp, 3 * width), BF16),
            shape_of((images, HEADS, sp, sp), BF16),
            shape_of((images, sp, width), BF16),
            shape_of((images, sp, width), F32),
            shape_of((images, sp, width), BF16),
            shape_of((images, sp, LANES), F32),
            shape_of((images, sp, LANES), F32),
        ]
        out_specs = [per_image(s.shape) for s in shapes] + slot_specs
        scratch = [pltpu.VMEM((images * WIDE, width + 2 * LANES), BF16)]
        if first:
            scratch.append(pltpu.VMEM((sp, width), F32))
        out = line(
            partial(
                forward_kernel,
                first=first,
                layer=layer,
                images=images,
                seq=seq,
                experts=experts,
                **dims,
            ),
            args,
            specs,
            out_specs,
            shapes + slot_shapes,
            (images,),
            scratch,
            cost(6e9, 2e7, 1e6),
            "forward",
        )
        state = tokens if first else out.pop(0)
        return state, out[:7], nested(out[7:])

    any_spec = pl.BlockSpec(memory_space=pl.ANY)

    def rows_of(lists, j, args, specs):
        for d in range(n):
            array = lists[d][j] if len(lists[d]) > 1 else lists[d][0]
            at = 0 if len(lists[d]) > 1 else j
            args.append(array)
            specs.append(spec((cp, width), lambda *_, at=at: (at, 0)))

    act_shape = shape_of((n * cp, hidden), BF16)
    act_spec = spec((n * cp, tile), lambda h, *_: (0, h))
    cat_shape = shape_of((n * cp, width), BF16)

    def run_expert(layer, j, x, g, made, produce, backward, earlier=()):
        args, specs = [ids], []
        rows_of(x, j, args, specs)
        if backward:
            rows_of(g, j, args, specs)
            if not produce:
                rows_of(made, j, args, specs)
        for parts in earlier:
            args += parts
            specs += [whole(slot_shape)] * n
        args += [w_in, w_out]
        specs += [
            spec((1, 1, width, tile), lambda h, who: (layer, who[1] * per + j, 0, h)),
            spec((1, 1, tile, width), lambda h, who: (layer, who[1] * per + j, h, 0)),
        ]
        shapes = []
        out_specs = []
        scratch = [pltpu.VMEM((n * cp, width), BF16)]
        if not backward:
            scratch.append(pltpu.VMEM((n * cp, tile), BF16))
        if produce:
            made_shape = shape_of(((1 + len(earlier)) * cp, width), BF16)
            shapes += [made_shape] * n
            out_specs += [whole(made_shape)] * n
            scratch += [pltpu.VMEM((n * cp, width), F32)]
        if backward:
            shapes += [slot_shape] * n + [act_shape] * 2 + [cat_shape]
            out_specs += [whole(slot_shape)] * n + [act_spec] * 2 + [whole(cat_shape)]
            scratch += [pltpu.VMEM((n * cp, width), BF16), pltpu.VMEM((n * cp, width), F32)]
        out = line(
            partial(
                expert_kernel,
                n=n,
                cp=cp,
                tiles=tiles,
                produce=produce,
                backward=backward,
                joined=len(earlier),
            ),
            args,
            specs,
            out_specs,
            shapes,
            (tiles,),
            scratch,
            cost(1, 1),
            "expert",
            1,
        )
        if backward:
            return out[:-3], out[-3:]
        return out, None

    def run_weights(j, x, saved, before=None, after=()):
        args, specs = [ids], []
        rows_of(x, j, args, specs)
        args += saved
        specs += [act_spec] * 2 + [whole(cat_shape)]
        aliases = {}
        if before is not None:
            aliases = {len(args): 0}
            args.append(before)
            specs.append(any_spec)
        return line(
            partial(
                weight_kernel,
                n=n,
                cp=cp,
                tiles=tiles,
                wire=(reps, rows_in, rows_out, j),
                follows=before is not None,
            ),
            args,
            specs,
            [any_spec],
            [shape_of((reps, 2 * per * rows_out, width), BF16)],
            (tiles,),
            [
                pltpu.VMEM((n * cp, width), BF16),
                pltpu.VMEM((reps, rows_out, width), BF16),
                pltpu.VMEM((reps, tiles * rows_in, tile), BF16),
                pltpu.SemaphoreType.DMA((2,)),
            ],
            cost(1, 1),
            "weights",
            1,
            after=after,
            aliases=aliases,
        )[0]

    def dense_steps(mine, other, result):
        parts = add(line, mine, swap(other, "rep", 1, reps))
        yield
        total = parts[0]
        for side in range(1, n_exp):
            total = add(line, total, swap(parts[side], "exp", side, n_exp))
            yield
        result.append(total)
        while True:
            yield

    def dense_over_chips(totals):
        chips = reps // cores
        parts = jnp.stack([t.reshape(chips, t.shape[0] // chips, t.shape[1]) for t in totals], axis=1)
        parts = lax.all_to_all(
            parts, "rep", split_axis=0, concat_axis=0, axis_index_groups=groups, tiled=True
        )
        share = jnp.sum(parts.astype(F32), axis=0, keepdims=True).astype(BF16)
        parts = lax.all_to_all(
            jnp.broadcast_to(share, parts.shape),
            "rep",
            split_axis=0,
            concat_axis=0,
            axis_index_groups=groups,
            tiled=True,
        )
        full = parts.transpose(1, 0, 2, 3).reshape(layers, totals[0].shape[0], totals[0].shape[1])
        return full, swap(full, "rep", 1, reps)

    def step(process):
        next(process, None)

    def run_out(previous):
        middle, gate, back = previous
        back = flat_of(back)
        return line(
            partial(out_kernel, seq=seq, **dims),
            [middle, gate, col] + back,
            [per_image(middle.shape), per_image(gate.shape), col_spec(top)] + [whole(p) for p in back],
            [per_image(tokens.shape)],
            [shape_of(tokens.shape, F32)],
            (images,),
            (),
            cost(2 * images * sp * n * per * cp * width, 6e6),
            "block_out",
        )[0]

    def run_backward(layer, grad, state, cached, d_back, carry):
        first = layer == 0
        last = layer == top
        joined, probs, attended, middle, moe_in, router, gate = cached
        args = [ids, grad, state, joined, probs, attended, middle, moe_in, router, col]
        specs = [smem()] + [per_image(a.shape) for a in args[1:-1]] + [col_spec(layer)]
        args += flat_of(d_back)
        specs += slot_specs
        args += [ln1_gain, ln1_bias, w_qkv, w_attn_out, ln2_gain, router_wide]
        specs += [
            whole(ln1_gain),
            whole(ln1_bias),
            of_layer(w_qkv, layer),
            of_layer(w_attn_out, layer),
            whole(ln2_gain),
            of_layer(router_wide, layer),
        ]
        dense_shape = shape_of((n_exp, width // n, 4 * width + LANES), BF16)
        grad_shape = tokens.shape if first else (images, sp, width)
        shapes = [shape_of(grad_shape, F32), dense_shape, dense_shape]
        out_specs = [per_image(grad_shape), whole(dense_shape), whole(dense_shape)]
        scratch = [
            pltpu.VMEM((n, per, cp, LANES), BF16),
            pltpu.VMEM((width, 3 * width), F32),
            pltpu.VMEM((width, width), F32),
            pltpu.VMEM((width, LANES), F32),
            pltpu.VMEM((8, width), F32),
            pltpu.VMEM((LANES, width), F32),
            pltpu.VMEM((sp, 3 * width), BF16),
        ]
        if last:
            scratch.append(pltpu.VMEM((sp, width), F32))
        if first:
            scratch.append(pltpu.VMEM((sp, width), F32))
        else:
            args.append(row)
            specs.append(row_spec_of(layer - 1))
            shapes += slot_shapes
            out_specs += slot_specs
            scratch.append(pltpu.VMEM((images * WIDE, width), BF16))
        out = line(
            partial(
                backward_kernel,
                first=first,
                last=last,
                layer=layer,
                images=images,
                seq=seq,
                experts=experts,
                **dims,
            ),
            args,
            specs,
            out_specs,
            shapes,
            (images,),
            scratch,
            cost(1.2e10, 3e7, 0),
            "backward",
            carry=carry,
        )
        count = len(out) - len(carry)
        return out[0], out[1:3], nested(out[3:count]), out[count:]

    kept = []
    previous = None
    for layer in range(layers):
        if layer == top:
            g_rows = send(spread_cotangent())
        state, cached, rows_sent = run_forward(layer, previous)
        x = send(rows_sent)
        made = [[] for _ in range(n)]
        if layer < top:
            for j in range(per):
                out, _ = run_expert(layer, j, x, None, None, True, False)
                for d in range(n):
                    made[d].append(out[d])
            previous = (cached[3], cached[6], send_back(made))
        kept.append((state, cached, x, made))

    state, cached, x, _ = kept[top]
    outs, saved = [], []
    d_back = [[] for _ in range(n)]
    for j in range(per):
        earlier = [o[:n] for o in outs] if j == per - 1 else ()
        out, kept_rows = run_expert(top, j, x, g_rows, None, True, True, earlier)
        outs.append(out)
        saved.append(kept_rows)
        for d, part in enumerate(out[n : 2 * n]):
            d_back[d].append(go_back(part, d))
    groups = [[r for r in range(reps) if r % cores == c] for c in range(cores)]

    def summed(x, saved):
        wire = None
        for j in range(per):
            wire = run_weights(j, x, saved[j], wire)
        share = lax.psum_scatter(
            wire, "rep", scatter_dimension=0, axis_index_groups=groups, tiled=True
        )
        half = share.shape[0] // 2
        return share[:half], swap(share[half:], "rep", 1, reps)

    shares = [None] * layers
    dense = [[] for _ in range(layers)]
    shares[top] = summed(x, saved)
    grad, parts, g_rows, _ = run_backward(top, cotangent, state, cached, d_back, ())
    g_rows = send(g_rows)
    flow_top = dense_steps(parts[0], parts[1], dense[top])
    back_top = send_back([[part] for part in outs[-1][:n]])
    block_out = run_out((cached[3], cached[6], back_top))

    state, cached, x, made = kept[0]
    d_back = [[] for _ in range(n)]
    saved = []
    for j in range(per):
        out, kept_rows = run_expert(0, j, x, g_rows, made, False, True)
        saved.append(kept_rows)
        for k in range(n):
            d_back[k].append(go_back(out[k], k))
        if j == 0:
            step(flow_top)
    shares[0] = summed(x, saved)
    grad, parts, _, _ = run_backward(0, grad, state, cached, d_back, ())
    flow = dense_steps(parts[0], parts[1], dense[0])
    step(flow)
    while not dense[top]:
        step(flow_top)
    while not dense[0]:
        step(flow)
    halves = list(dense_over_chips([d[0] for d in dense]))
    rows = width // n_exp
    dense_shapes = [
        shape_of((layers, rows, 3 * width), F32),
        shape_of((layers, rows, width), F32),
        shape_of((layers, rows, experts), F32),
    ] + [shape_of((layers, rows), F32)] * 4
    qkv, attn_out, router, gain1, bias1, gain2, bias2 = line(
        partial(dense_kernel, layers=layers, width=width, experts=experts),
        [ids] + halves,
        [smem()] + [whole(p) for p in halves],
        [whole(s) for s in dense_shapes],
        dense_shapes,
        (1,),
        [pltpu.VMEM((WIDE, LANES), F32)],
        cost(1e6, 6e6),
        "finish_dense",
    )
    pieces = [part for pair in shares for part in pair]
    in_shape = shape_of((layers, local_experts, rows_in, hidden), F32)
    out_shape = shape_of((layers, local_experts, rows_out, width), F32)
    grad_in, grad_out = line(
        partial(finish_kernel, layers=layers, pairs=per, tiles=tiles, rows_in=rows_in),
        [ids] + pieces,
        [smem()] + [whole(p) for p in pieces],
        [whole(in_shape), whole(out_shape)],
        [in_shape, out_shape],
        (1,),
        (),
        cost(1e6, 6e6),
        "finish",
    )
    return (
        block_out,
        grad,
        gain1,
        bias1,
        qkv,
        attn_out,
        gain2,
        bias2,
        router,
        grad_in,
        grad_out,
    )


def solution(mesh):
    return jax.shard_map(
        partial(local, n_exp=mesh.shape["exp"], reps=mesh.shape["rep"]),
        mesh=mesh,
        in_specs=(
            P(("rep", "exp"), None, None),
            P(),
            P(),
            P(),
            P(),
            P(),
            P(),
            P(),
            P(None, "exp", None, None),
            P(None, "exp", None, None),
            P(None, ("rep", "exp"), None),
            P(None, ("rep", "exp"), None),
            P(("rep", "exp"), None, None),
        ),
        out_specs=(
            P(("rep", "exp"), None, None),
            P(("rep", "exp"), None, None),
            P(None, "exp"),
            P(None, "exp"),
            P(None, "exp", None),
            P(None, "exp", None),
            P(None, "exp"),
            P(None, "exp"),
            P(None, "exp", None),
            P(None, "exp", "rep", None),
            P(None, "exp", "rep", None),
        ),
        check_vma=False,
    )
```
